32 devices in a mesh: groups: 2 (over x), brick: 4 (over y, core), tm: 4 (over z).
Axes of the slice: x: 2, y: 2, z: 4, core: 2. Of those that a mesh axis runs over, the one named last changes fastest.
Arguments:
- link_rows: float32 [8, 2, 2, 3, 8, 8, 768], P('groups', None, None, None, 'brick', 'tm'), parts along dimension 0, may hold values from -1 to 1, as said below
- target: float32 [8, 8, 8, 8, 768], P('groups', None, 'brick', 'tm'), parts along dimension 0, may hold values from -6 to 6
- weights: float32 [4, 6], replicated, may hold values from -3 to 3
Outputs:
- weight_grad: float32 [8, 6], P('groups'), parts along dimension 0
- link_force: float32 [8, 8, 8, 8, 768], P('groups', None, 'brick', 'tm'), parts along dimension 0
The draws below stay inside these ranges and needn't reach their ends.
There are 2 independent parts, one for each index of `groups`. The reference program is written for one: setup_inputs(seed, part) draws one part's arguments, and reference() takes and returns one part's arrays. A program takes and returns all parts, laid end to end along the dimension named above; an argument that names none is the same for every part. Nothing has to cross between parts.
Inputs may be any that keep to these rules, and one draw needn't show every extreme that they name: `link_rows`: the two rows of each link are orthonormal complex vectors, so every rebuilt link is special unitary.
All inputs are finite; a program needn't handle non-finite values.
Results may differ from the reference program's by a relative error of at most 0.0003.
Values sent between devices are 32-bit elements; how exact they have to be, the bound alone decides.
A program may use at most 256 MiB of HBM per device.

```python
from functools import partial
import jax
import jax.numpy as jnp
from jax import lax

NY = 48
NZ = 16
NX = 8
NT = 8


def draw_link_rows(key, part):
    key = jax.random.fold_in(key, 11)
    shape = (4, 2, 2, 3, NX, NT, NY * NZ)
    noise = jnp.clip(0.5 * jax.random.normal(key, shape, jnp.float32), -1.0, 1.0)
    along_x = lax.broadcasted_iota(jnp.float32, (NX, NT, NY * NZ), 0) / NX
    along_t = lax.broadcasted_iota(jnp.float32, (NX, NT, NY * NZ), 1) / NT
    spread = 0.3 + 0.5 * along_x + 0.4 * along_t
    base = jnp.zeros((2, 2, 3), jnp.float32).at[0, 0, 0].set(1.0).at[0, 1, 1].set(1.0)
    rows = 1.5 * base[None, :, :, :, None, None, None] + spread * noise
    row_one = rows[:, :, 0]
    row_two = rows[:, :, 1]
    length_one = jnp.sqrt(jnp.sum(row_one * row_one, axis=(1, 2), keepdims=True))
    row_one = row_one / length_one
    inner_real = jnp.sum(row_one[:, 0] * row_two[:, 0] + row_one[:, 1] * row_two[:, 1], axis=1, keepdims=True)
    inner_imag = jnp.sum(row_one[:, 0] * row_two[:, 1] - row_one[:, 1] * row_two[:, 0], axis=1, keepdims=True)
    along_real = inner_real * row_one[:, 0] - inner_imag * row_one[:, 1]
    along_imag = inner_real * row_one[:, 1] + inner_imag * row_one[:, 0]
    row_two = row_two - jnp.stack([along_real, along_imag], 1)
    length_two = jnp.sqrt(jnp.sum(row_two * row_two, axis=(1, 2), keepdims=True))
    row_two = row_two / length_two
    return jnp.stack([row_one, row_two], 2).astype(jnp.float32)


def shard_levels(stream_key, shape, split, smallest, largest):
    gain, own = 1.0, jax.random.fold_in(stream_key, 6)
    for axis_at, parts in split:
        steps = jnp.exp(jax.random.uniform(jax.random.fold_in(own, axis_at), (parts,), jnp.float32, smallest / len(split), largest / len(split)))
        gain = gain * jnp.repeat(steps, shape[axis_at] // parts).reshape([-1 if axis == axis_at else 1 for axis in range(len(shape))])
    return gain


def scatter_about(stream_key, shape, width, reach, split=(), dtype=jnp.bfloat16):
    drawn = width * jax.random.normal(stream_key, shape, jnp.float32)
    if split:
        drawn = drawn * shard_levels(stream_key, shape, split, -0.22, 0.18)
    return jnp.clip(drawn, -reach, reach).astype(dtype)


def setup_inputs(seed: int = 0, part: int = 0) -> dict:
    keys = jax.random.split(jax.random.key(seed), 4)
    part_keys = jax.random.split(jax.random.fold_in(keys[3], part), 4)
    link_rows = draw_link_rows(jax.random.fold_in(jax.random.fold_in(keys[3], part), 71), part)
    target = scatter_about(part_keys[1], (4, 8, NX, NT, NY * NZ), 1.0, 6.0, ((2, 4), (3, 4)), jnp.float32)
    weights = scatter_about(keys[2], (4, 6), 0.5, 3.0, (), jnp.float32)
    return {"link_rows": link_rows, "target": target, "weights": weights}


ROOT_THREE = 3.0 ** 0.5

def small_product(left, right):
    total = left[:, 0][:, None] * right[0][None, :]
    total = total + left[:, 1][:, None] * right[1][None, :]
    return total + left[:, 2][:, None] * right[2][None, :]

def complex_product(first_matrix, second_matrix):
    real_part = small_product(first_matrix[0], second_matrix[0]) - small_product(first_matrix[1], second_matrix[1])
    imag_part = small_product(first_matrix[0], second_matrix[1]) + small_product(first_matrix[1], second_matrix[0])
    return jnp.stack([real_part, imag_part])

def dagger(matrix):
    return jnp.stack([jnp.swapaxes(matrix[0], 0, 1), -jnp.swapaxes(matrix[1], 0, 1)])

def entry_product(left, right):
    return (left[:, 0] * right[:, 0] - left[:, 1] * right[:, 1], left[:, 0] * right[:, 1] + left[:, 1] * right[:, 0])

def complete(two_rows):
    row_one = two_rows[:, :, 0]
    row_two = two_rows[:, :, 1]
    cross_real, cross_imag = ([], [])
    for i, j in ((1, 2), (2, 0), (0, 1)):
        ahead_real, ahead_imag = entry_product(row_one[:, :, i], row_two[:, :, j])
        behind_real, behind_imag = entry_product(row_one[:, :, j], row_two[:, :, i])
        cross_real.append(ahead_real - behind_real)
        cross_imag.append(behind_imag - ahead_imag)
    third_row = jnp.stack([jnp.stack(cross_real, 1), jnp.stack(cross_imag, 1)], 1)
    return jnp.concatenate([two_rows, third_row[:, :, None]], axis=2)

def algebra(matrix):
    real_part, imag_part = (matrix[0], matrix[1])
    return jnp.stack([imag_part[0, 1] + imag_part[1, 0], real_part[0, 1] - real_part[1, 0], imag_part[0, 0] - imag_part[1, 1], imag_part[0, 2] + imag_part[2, 0], real_part[0, 2] - real_part[2, 0], imag_part[1, 2] + imag_part[2, 1], real_part[1, 2] - real_part[2, 1], (imag_part[0, 0] + imag_part[1, 1] - 2.0 * imag_part[2, 2]) / ROOT_THREE])

def move_plane(matrix, step_y, step_z):
    if step_y != 0:
        matrix = jnp.roll(matrix, -step_y * NZ, axis=-1)
    if step_z != 0:
        column = lax.broadcasted_iota(jnp.int32, (matrix.shape[-1],), 0) % NZ
        edge = NZ - 1 if step_z > 0 else 0
        inside = jnp.roll(matrix, -step_z, axis=-1)
        across = jnp.roll(matrix, step_z * (NZ - 1), axis=-1)
        matrix = jnp.where(column == edge, across, inside)
    return matrix

def rolled(link_field, direction, step):
    matrix = link_field[direction]
    matrix = jnp.roll(matrix, -step[0], axis=3)
    matrix = jnp.roll(matrix, -step[3], axis=4)
    return move_plane(matrix, step[1], step[2])

def offset(direction, sign):
    return tuple((sign if k == direction else 0 for k in range(4)))

def step_sum(left, right):
    return tuple((left[k] + right[k] for k in range(4)))

def staple_pair(link_field, weights, direction, other, position, shifted_at):
    forward = offset(direction, 1)
    here = (0, 0, 0, 0)
    side = offset(other, 1)
    back_side = offset(other, -1)
    upper_staple = complex_product(complex_product(shifted_at(link_field, other, forward), dagger(shifted_at(link_field, direction, side))), dagger(shifted_at(link_field, other, here)))
    lower_staple = complex_product(complex_product(dagger(shifted_at(link_field, other, step_sum(forward, back_side))), dagger(shifted_at(link_field, direction, back_side))), shifted_at(link_field, other, back_side))
    return weights[direction, 2 * position] * upper_staple + weights[direction, 2 * position + 1] * lower_staple

def one_direction(link_field, weights, direction, shifted_at):
    here = (0, 0, 0, 0)
    staple_sum = 0.0
    others = [k for k in range(4) if k != direction]
    for j in range(3):
        pair_fn = jax.checkpoint(partial(staple_pair, direction=direction, other=others[j], position=j, shifted_at=shifted_at))
        staple_sum = staple_sum + pair_fn(link_field, weights)
    loop_matrix = complex_product(shifted_at(link_field, direction, here), staple_sum)
    return algebra(loop_matrix)

def velocity(link_field, weights, shifted_at):
    return jnp.stack([jax.checkpoint(partial(one_direction, direction=k, shifted_at=shifted_at))(link_field, weights) for k in range(4)])

def project_force(link_field, grad_field):
    return jnp.stack([-algebra(complex_product(link_field[k], dagger(grad_field[k]))) for k in range(4)])

def reference(link_rows, target, weights):
    link_field = complete(link_rows)

    def loss_value(field, values):
        difference = velocity(field, values, rolled) - target
        return 0.5 * jnp.sum(difference * difference)
    grad_field, grad_weights = jax.grad(loss_value, argnums=(0, 1))(link_field, weights)
    link_force = project_force(link_field, grad_field)
    return (grad_weights / (NX * NY * NZ * NT), link_force)
```

```python
import jax
import jax.numpy as jnp
from jax import lax
from jax.experimental import pallas as pl
from jax.experimental.pallas import tpu as pltpu
from jax.sharding import PartitionSpec as P

NZ = 16
LANES = 128
ROOT_THREE = 3.0**0.5
VMEM = pl.BlockSpec(memory_space=pltpu.VMEM)
SMEM = pl.BlockSpec(memory_space=pltpu.SMEM)


def mul(a, b):
    return a[0] * b[0] - a[1] * b[1], a[0] * b[1] + a[1] * b[0]


def mul_conj(a, b):
    return a[0] * b[0] + a[1] * b[1], a[1] * b[0] - a[0] * b[1]


def add(*terms):
    re, im = terms[0]
    for t in terms[1:]:
        re, im = re + t[0], im + t[1]
    return re, im


def sub(a, b):
    return a[0] - b[0], a[1] - b[1]


def conj(a):
    return a[0], -a[1]


def scale(a, s):
    return a[0] * s, a[1] * s


def cross_row(r, s):
    out = []
    for i, j in ((1, 2), (2, 0), (0, 1)):
        out.append(conj(sub(mul(r[i], s[j]), mul(r[j], s[i]))))
    return out


def product(a, b):
    rows = [
        [add(mul(a[i][0], b[0][k]), mul(a[i][1], b[1][k]), mul(a[i][2], b[2][k])) for k in range(3)]
        for i in range(2)
    ]
    return rows + [cross_row(*rows)]


def product_dagger(a, b):
    rows = [
        [
            add(mul_conj(a[i][0], b[k][0]), mul_conj(a[i][1], b[k][1]), mul_conj(a[i][2], b[k][2]))
            for k in range(3)
        ]
        for i in range(2)
    ]
    return rows + [cross_row(*rows)]


def dagger(a):
    return [[conj(a[j][i]) for j in range(3)] for i in range(3)]


def conjugated(u, h):
    d0, d1, h01, h02, h12 = h
    t = []
    for i in range(2):
        a, b, c = u[i]
        t.append(
            [
                add(scale(a, d0), mul_conj(b, h01), mul_conj(c, h02)),
                add(scale(b, d1), mul(a, h01), mul_conj(c, h12)),
                add(mul(a, h02), mul(b, h12)),
            ]
        )

    def entry(i, j):
        return add(*[mul_conj(t[i][k], u[j][k]) for k in range(3)])

    def diagonal(i):
        return sum(t[i][k][0] * u[i][k][0] + t[i][k][1] * u[i][k][1] for k in range(3))

    e0, e1 = diagonal(0), diagonal(1)
    e2 = d0 + d1 - e0 - e1
    return e0 - e2, e1 - e2, entry(0, 1), entry(0, 2), entry(1, 2)


def flat(h):
    d0, d1, a, b, c = h
    return [d0, d1, *a, *b, *c]


def unflat(v):
    return v[0], v[1], (v[2], v[3]), (v[4], v[5]), (v[6], v[7])


def hermitian_part(p):
    return (
        [p[k][k][0] for k in range(3)],
        *[
            (0.5 * (p[i][j][0] + p[j][i][0]), 0.5 * (p[i][j][1] - p[j][i][1]))
            for i, j in ((0, 1), (0, 2), (1, 2))
        ],
    )


def anti_part(p):
    d = [p[k][k][1] for k in range(3)]
    return (
        d[0] - d[2],
        d[1] - d[2],
        *[
            (0.5 * (p[i][j][1] + p[j][i][1]), 0.5 * (p[j][i][0] - p[i][j][0]))
            for i, j in ((0, 1), (0, 2), (1, 2))
        ],
    )


def half_anticommutator(pr, q):
    p, p01, p02, p12 = pr
    d0, d1, q01, q02, q12 = q
    mean = (d0 + d1) * (1.0 / 3.0)
    q0, q1, q2 = d0 - mean, d1 - mean, -mean
    e01 = add(scale(q01, p[0] + p[1]), scale(p01, -q2), mul_conj(p02, q12), mul_conj(q02, p12))
    e02 = add(scale(q02, p[0] + p[2]), scale(p02, -q1), mul(p01, q12), mul(q01, p12))
    e12 = add(scale(q12, p[1] + p[2]), scale(p12, -q0), mul_conj(q02, p01), mul_conj(p02, q01))
    x01 = p01[0] * q01[0] + p01[1] * q01[1]
    x02 = p02[0] * q02[0] + p02[1] * q02[1]
    x12 = p12[0] * q12[0] + p12[1] * q12[1]
    last = p[2] * q2
    return (
        p[0] * q0 - last + x01 - x12,
        p[1] * q1 - last + x01 - x02,
        scale(e01, 0.5),
        scale(e02, 0.5),
        scale(e12, 0.5),
    )


def i_commutator(x, y):
    x0, x1, x01, x02, x12 = x
    y0, y1, y01, y02, y12 = y
    c01 = sub(add(scale(y01, x0 - x1), scale(x01, y1 - y0), mul_conj(x02, y12)), mul_conj(y02, x12))
    c02 = sub(add(scale(y02, x0), scale(x02, -y0), mul(x01, y12)), mul(y01, x12))
    c12 = sub(add(scale(y12, x1), scale(x12, -y1), mul_conj(y02, x01)), mul_conj(x02, y01))
    a01 = x01[1] * y01[0] - x01[0] * y01[1]
    a02 = x02[1] * y02[0] - x02[0] * y02[1]
    a12 = x12[1] * y12[0] - x12[0] * y12[1]
    d2 = 2.0 * (a02 + a12)
    return (
        -2.0 * (a01 + a02) - d2,
        2.0 * (a01 - a12) - d2,
        (-c01[1], c01[0]),
        (-c02[1], c02[0]),
        (-c12[1], c12[0]),
    )


def plane(p):
    mu = jnp.where(p < 3, 0, jnp.where(p < 5, 1, 2))
    nu = jnp.where(p < 3, p + 1, jnp.where(p < 5, p - 1, 3))
    return mu, nu


PLANES = ((0, 1), (0, 2), (0, 3), (1, 2), (1, 3), (2, 3))


def grid_of(shape):
    lane = lax.broadcasted_iota(jnp.int32, shape, 1)
    row = lax.broadcasted_iota(jnp.int32, shape, 0)
    return row, lane


def move_z(v, step):
    row, lane = grid_of(v.shape)
    inside = pltpu.roll(v, (-step) % LANES, 1)
    across = pltpu.roll(v, (step * (NZ - 1)) % LANES, 1)
    edge = NZ - 1 if step > 0 else 0
    return jnp.where(lane % NZ == edge, across, inside)


def move_y(v, step, per_cell):
    rows = v.shape[0]
    row, lane = grid_of(v.shape)
    turned = pltpu.roll(v, (-step * NZ) % LANES, 1)
    inside = pltpu.roll(turned, (-step) % rows, 0)
    across = pltpu.roll(turned, (step * (per_cell - 1)) % rows, 0)
    edge = per_cell - 1 if step > 0 else 0
    other = jnp.where(row % per_cell == edge, across, inside)
    over = lane >= LANES - NZ if step > 0 else lane < NZ
    return jnp.where(over, other, turned)


def load_matrix(ref, index, rows):
    at = lambda c: ref[(*index, c, rows, slice(None))]
    return [[(at(3 * i + j), at(9 + 3 * i + j)) for j in range(3)] for i in range(3)]


def store_matrix(ref, index, rows, m):
    for i in range(3):
        for j in range(3):
            for part in range(2):
                ref[(*index, 9 * part + 3 * i + j, rows, slice(None))] = m[i][j][part]


def load_flat(ref, index, rows):
    return unflat([ref[(*index, c, rows, slice(None))] for c in range(8)])


def store_flat(ref, index, rows, h):
    for c, v in enumerate(flat(h)):
        ref[(*index, c, rows, slice(None))] = v


def add_flat(ref, index, rows, h):
    for c, v in enumerate(flat(h)):
        ref[(*index, c, rows, slice(None))] += v


def complete_into(src, src_index, dst, dst_index, total):
    def chunk(k, carry):
        rows = pl.ds(pl.multiple_of(8 * k, 8), 8)
        at = lambda c: src[(*src_index, c, rows, slice(None))]
        m = [[(at(3 * i + j), at(6 + 3 * i + j)) for j in range(3)] for i in range(2)]
        m.append(cross_row(*m))
        store_matrix(dst, dst_index, rows, m)
        return carry

    lax.fori_loop(0, total // 8, chunk, 0)


def loops_kernel(per_cell, own, along_x, along_t, plaq, here, moved_b, moved_c, full):
    total = own.shape[2]
    for d in range(4):
        complete_into(own, (d,), full, (0, d), total)
    for k in range(3):
        complete_into(along_x, (k,), full, (1, k + 1), total)
        complete_into(along_t, (k,), full, (4, k), total)

    def shift_links(c, carry):
        for d in range(4):
            value = full[0, d, c]
            if d != 1:
                full[2, d, c] = move_y(value, 1, per_cell)
            if d != 2:
                full[3, d, c] = move_z(value, 1)
        return carry

    lax.fori_loop(0, 18, shift_links, 0)
    chunks = total // 8

    def step(i, carry):
        p = i // chunks
        rows = pl.ds(pl.multiple_of(8 * (i % chunks), 8), 8)
        mu, nu = plane(p)
        a = load_matrix(full, (0, mu), rows)
        b = load_matrix(full, (1 + mu, nu), rows)
        c = load_matrix(full, (1 + nu, mu), rows)
        d = load_matrix(full, (0, nu), rows)
        loop = product_dagger(product(a, b), product(d, c))
        store_matrix(plaq, (p,), rows, loop)
        pi = anti_part(loop)
        store_flat(here, (p,), rows, pi)
        store_flat(moved_b, (p,), rows, conjugated(dagger(a), pi))
        store_flat(moved_c, (p,), rows, conjugated(dagger(d), pi))
        return carry

    lax.fori_loop(0, 6 * chunks, step, 0)

    def shift_back(c, carry):
        for p in (3, 4):
            moved_b[p, c] = move_y(moved_b[p, c], -1, per_cell)
        moved_b[5, c] = move_z(moved_b[5, c], -1)
        moved_c[0, c] = move_y(moved_c[0, c], -1, per_cell)
        for p in (1, 3):
            moved_c[p, c] = move_z(moved_c[p, c], -1)
        return carry

    lax.fori_loop(0, 8, shift_back, 0)


def residual_kernel(weights, target, here, moved_b, moved_c, from_x, from_t, residual, sums):
    total = target.shape[2]

    def chunk(k, carry):
        rows = pl.ds(pl.multiple_of(8 * k, 8), 8)
        acc = []
        for mu in range(4):
            terms = []
            for j in range(3):
                nu = [n for n in range(4) if n != mu][j]
                p = PLANES.index((min(mu, nu), max(mu, nu)))
                load = lambda ref, index: [ref[index, c, rows, :] for c in range(8)]
                if mu < nu:
                    sign = 1.0
                    up = load(here, p)
                    low = load(from_t, (2, 4, 5).index(p)) if nu == 3 else load(moved_c, p)
                else:
                    sign = -1.0
                    up = load(here, p)
                    low = load(from_x, p) if nu == 0 else load(moved_b, p)
                terms.append((sign, up))
                terms.append((-sign, low))
            v = [
                sum(terms[s][1][c] * (terms[s][0] * weights[mu, s]) for s in range(6))
                for c in range(8)
            ]
            t = [target[mu, a, rows, :] for a in range(8)]
            r3 = v[0] - v[1] - t[2]
            r8 = (v[0] + v[1]) * (1.0 / ROOT_THREE) - t[7]
            r = [
                r3 + ROOT_THREE * r8,
                ROOT_THREE * r8 - r3,
                2.0 * v[2] - t[0],
                2.0 * v[3] + t[1],
                2.0 * v[4] - t[3],
                2.0 * v[5] + t[4],
                2.0 * v[6] - t[5],
                2.0 * v[7] + t[6],
            ]
            for c in range(8):
                residual[mu, c, rows, :] = r[c]
            g = [r3 + r8 * (1.0 / ROOT_THREE), r8 * (1.0 / ROOT_THREE) - r3]
            g += [2.0 * x for x in r[2:]]
            for sign, w in terms:
                acc.append(sign * sum(g[c] * w[c] for c in range(8)))
        return tuple(x + y for x, y in zip(carry, acc))

    zero = jnp.zeros((8, LANES), jnp.float32)
    acc = lax.fori_loop(0, total // 8, chunk, (zero,) * 24)
    for n, x in enumerate(acc):
        sums[n : n + 1, :] = jnp.sum(x, axis=0, keepdims=True)


def force_kernel(
    per_cell, weights, own, plaq, residual, along_x, along_t, force, to_x, to_t, full, res, back_b, back_c
):
    total = own.shape[2]
    for d in range(4):
        complete_into(own, (d,), full, (d,), total)

    def shift_residual(c, carry):
        for d in range(4):
            value = residual[d, c]
            res[0, d, c] = value
            if d != 1:
                res[2, d, c] = move_y(value, 1, per_cell)
            if d != 2:
                res[3, d, c] = move_z(value, 1)
            force[d, c] = jnp.zeros_like(value)
        for k in range(3):
            res[1, k + 1, c] = along_x[k, c]
            res[4, k, c] = along_t[k, c]
        return carry

    lax.fori_loop(0, 8, shift_residual, 0)
    chunks = total // 8

    def step(i, carry):
        p = i // chunks
        rows = pl.ds(pl.multiple_of(8 * (i % chunks), 8), 8)
        mu, nu = plane(p)
        wa, wc = weights[mu, 2 * (nu - 1)], weights[mu, 2 * (nu - 1) + 1]
        wd, wb = weights[nu, 2 * mu], weights[nu, 2 * mu + 1]
        a = load_matrix(full, (mu,), rows)
        d = load_matrix(full, (nu,), rows)
        loop = load_matrix(plaq, (p,), rows)
        pr, pi = hermitian_part(loop), anti_part(loop)
        sb = [x * wb for x in flat(conjugated(a, load_flat(res, (1 + mu, nu), rows)))]
        sc = [x * wc for x in flat(conjugated(d, load_flat(res, (1 + nu, mu), rows)))]
        ra = flat(load_flat(res, (0, mu), rows))
        rd = flat(load_flat(res, (0, nu), rows))
        q = unflat([wa * ra[c] - wd * rd[c] + sb[c] - sc[c] for c in range(8)])
        e = flat(half_anticommutator(pr, q))
        k = [0.5 * x for x in flat(i_commutator(pi, q))]
        fore = [x + y for x, y in zip(e, k)]
        aft = [y - x for x, y in zip(e, k)]
        store_flat(back_b, (p,), rows, conjugated(dagger(a), unflat(fore)))
        store_flat(back_c, (p,), rows, conjugated(dagger(d), unflat(aft)))
        xb = flat(i_commutator(pi, unflat(sb)))
        xc = flat(i_commutator(pi, unflat(sc)))
        add_flat(force, (mu,), rows, unflat([x - y for x, y in zip(fore, xb)]))
        add_flat(force, (nu,), rows, unflat([x + y for x, y in zip(aft, xc)]))
        return carry

    lax.fori_loop(0, 6 * chunks, step, 0)

    def shift_back(c, carry):
        for k in range(3):
            to_x[k, c] = back_b[k, c]
            to_t[k, c] = back_c[(2, 4, 5)[k], c]
        force[2, c] += move_y(back_b[3, c], -1, per_cell)
        force[3, c] += move_y(back_b[4, c], -1, per_cell) + move_z(back_b[5, c], -1)
        force[0, c] += move_y(back_c[0, c], -1, per_cell) + move_z(back_c[1, c], -1)
        force[1, c] += move_z(back_c[3, c], -1)
        return carry

    lax.fori_loop(0, 8, shift_back, 0)


def body(link_rows, target, weights):
    f32 = jnp.float32
    nx, nt, plane_sites = link_rows.shape[4:]
    bricks, tms = lax.axis_size("brick"), lax.axis_size("tm")
    sites = nx * nt * plane_sites
    total = sites // LANES
    per_cell = plane_sites // LANES
    size = lambda *lead: jax.ShapeDtypeStruct((*lead, total, LANES), f32)
    params = pltpu.CompilerParams(vmem_limit_bytes=48 * 1024 * 1024)

    def ahead(values, axis, dim):
        dim = values.ndim - dim
        n = lax.axis_size(axis)
        first = lax.slice_in_dim(values, 0, 1, axis=dim)
        rest = lax.slice_in_dim(values, 1, values.shape[dim], axis=dim)
        first = lax.ppermute(first, axis, [((i + 1) % n, i) for i in range(n)])
        return jnp.concatenate([rest, first], axis=dim)

    def behind(values, axis, dim):
        dim = values.ndim - dim
        n = lax.axis_size(axis)
        extent = values.shape[dim]
        last = lax.slice_in_dim(values, extent - 1, extent, axis=dim)
        rest = lax.slice_in_dim(values, 0, extent - 1, axis=dim)
        last = lax.ppermute(last, axis, [(i, (i + 1) % n) for i in range(n)])
        return jnp.concatenate([last, rest], axis=dim)

    def spread(values):
        return values.reshape(*values.shape[:-2], nx, nt, plane_sites)

    def packed(values, count):
        return values.reshape(-1, count, total, LANES)

    own = packed(link_rows, 12)
    links_x = packed(ahead(link_rows[1:4], "brick", 3), 12)
    links_t = packed(ahead(link_rows[0:3], "tm", 2), 12)
    plaq, here, moved_b, moved_c = pl.pallas_call(
        lambda *refs: loops_kernel(per_cell, *refs),
        out_shape=(size(6, 18), size(6, 8), size(6, 8), size(6, 8)),
        in_specs=[VMEM] * 3,
        out_specs=(VMEM,) * 4,
        scratch_shapes=[pltpu.VMEM((5, 4, 18, total, LANES), f32)],
        compiler_params=params,
        name="loops",
    )(own, links_x, links_t)
    from_x = packed(behind(spread(moved_b[0:3]), "brick", 3), 8)
    from_t = packed(
        behind(spread(jnp.stack([moved_c[2], moved_c[4], moved_c[5]])), "tm", 2), 8
    )
    residual, sums = pl.pallas_call(
        residual_kernel,
        out_shape=(size(4, 8), jax.ShapeDtypeStruct((24, LANES), f32)),
        in_specs=[SMEM] + [VMEM] * 6,
        out_specs=(VMEM, VMEM),
        compiler_params=params,
        name="residual",
    )(weights, packed(target, 8), here, moved_b, moved_c, from_x, from_t)
    weight_grad = lax.psum(jnp.sum(sums, axis=1).reshape(4, 6), ("brick", "tm"))
    weight_grad = weight_grad / (sites * bricks * tms)
    res_x = packed(ahead(spread(residual[1:4]), "brick", 3), 8)
    res_t = packed(ahead(spread(residual[0:3]), "tm", 2), 8)
    force, to_x, to_t = pl.pallas_call(
        lambda *refs: force_kernel(per_cell, *refs),
        out_shape=(size(4, 8), size(3, 8), size(3, 8)),
        in_specs=[SMEM] + [VMEM] * 5,
        out_specs=(VMEM,) * 3,
        scratch_shapes=[
            pltpu.VMEM((4, 18, total, LANES), f32),
            pltpu.VMEM((5, 4, 8, total, LANES), f32),
            pltpu.VMEM((6, 8, total, LANES), f32),
            pltpu.VMEM((6, 8, total, LANES), f32),
        ],
        compiler_params=params,
        name="force",
    )(weights, own, plaq, residual, res_x, res_t)
    f = spread(force)
    fx = behind(spread(to_x), "brick", 3)
    ft = behind(spread(to_t), "tm", 2)
    zero = jnp.zeros_like(fx[:1])
    h = f + jnp.concatenate([zero, fx]) + jnp.concatenate([ft, zero])
    link_force = jnp.stack(
        [
            2.0 * h[:, 2],
            -2.0 * h[:, 3],
            h[:, 0] - h[:, 1],
            2.0 * h[:, 4],
            -2.0 * h[:, 5],
            2.0 * h[:, 6],
            -2.0 * h[:, 7],
            (h[:, 0] + h[:, 1]) * (1.0 / ROOT_THREE),
        ],
        axis=1,
    )
    return weight_grad, link_force


def solution(mesh):
    in_specs = (
        P("groups", None, None, None, "brick", "tm", None),
        P("groups", None, "brick", "tm", None),
        P(),
    )
    out_specs = (P("groups", None), P("groups", None, "brick", "tm", None))
    return jax.shard_map(body, mesh=mesh, in_specs=in_specs, out_specs=out_specs, check_vma=False)
```

```python
import jax
import jax.numpy as jnp
from jax import lax
from jax.experimental import pallas as pl
from jax.experimental.pallas import tpu as pltpu
from jax.sharding import PartitionSpec as P

NZ = 16
LANES = 128
ROOT_THREE = 3.0**0.5
VMEM = pl.BlockSpec(memory_space=pltpu.VMEM)
SMEM = pl.BlockSpec(memory_space=pltpu.SMEM)


def mul(a, b):
    return a[0] * b[0] - a[1] * b[1], a[0] * b[1] + a[1] * b[0]


def mul_conj(a, b):
    return a[0] * b[0] + a[1] * b[1], a[1] * b[0] - a[0] * b[1]


def add(*terms):
    re, im = terms[0]
    for t in terms[1:]:
        re, im = re + t[0], im + t[1]
    return re, im


def sub(a, b):
    return a[0] - b[0], a[1] - b[1]


def conj(a):
    return a[0], -a[1]


def scale(a, s):
    return a[0] * s, a[1] * s


def cross_row(r, s):
    out = []
    for i, j in ((1, 2), (2, 0), (0, 1)):
        out.append(conj(sub(mul(r[i], s[j]), mul(r[j], s[i]))))
    return out


def product(a, b):
    rows = [
        [add(mul(a[i][0], b[0][k]), mul(a[i][1], b[1][k]), mul(a[i][2], b[2][k])) for k in range(3)]
        for i in range(2)
    ]
    return rows + [cross_row(*rows)]


def product_dagger(a, b):
    rows = [
        [
            add(mul_conj(a[i][0], b[k][0]), mul_conj(a[i][1], b[k][1]), mul_conj(a[i][2], b[k][2]))
            for k in range(3)
        ]
        for i in range(2)
    ]
    return rows + [cross_row(*rows)]


def dagger(a):
    return [[conj(a[j][i]) for j in range(3)] for i in range(3)]


def conjugated(u, h):
    d0, d1, h01, h02, h12 = h
    t = []
    for i in range(2):
        a, b, c = u[i]
        t.append(
            [
                add(scale(a, d0), mul_conj(b, h01), mul_conj(c, h02)),
                add(scale(b, d1), mul(a, h01), mul_conj(c, h12)),
                add(mul(a, h02), mul(b, h12)),
            ]
        )

    def entry(i, j):
        return add(*[mul_conj(t[i][k], u[j][k]) for k in range(3)])

    def diagonal(i):
        return sum(t[i][k][0] * u[i][k][0] + t[i][k][1] * u[i][k][1] for k in range(3))

    e0, e1 = diagonal(0), diagonal(1)
    e2 = d0 + d1 - e0 - e1
    return e0 - e2, e1 - e2, entry(0, 1), entry(0, 2), entry(1, 2)


def flat(h):
    d0, d1, a, b, c = h
    return [d0, d1, *a, *b, *c]


def unflat(v):
    return v[0], v[1], (v[2], v[3]), (v[4], v[5]), (v[6], v[7])


def hermitian_part(p):
    return (
        [p[k][k][0] for k in range(3)],
        *[
            (0.5 * (p[i][j][0] + p[j][i][0]), 0.5 * (p[i][j][1] - p[j][i][1]))
            for i, j in ((0, 1), (0, 2), (1, 2))
        ],
    )


def anti_part(p):
    d = [p[k][k][1] for k in range(3)]
    return (
        d[0] - d[2],
        d[1] - d[2],
        *[
            (0.5 * (p[i][j][1] + p[j][i][1]), 0.5 * (p[j][i][0] - p[i][j][0]))
            for i, j in ((0, 1), (0, 2), (1, 2))
        ],
    )


def half_anticommutator(pr, q):
    p, p01, p02, p12 = pr
    d0, d1, q01, q02, q12 = q
    mean = (d0 + d1) * (1.0 / 3.0)
    q0, q1, q2 = d0 - mean, d1 - mean, -mean
    e01 = add(scale(q01, p[0] + p[1]), scale(p01, -q2), mul_conj(p02, q12), mul_conj(q02, p12))
    e02 = add(scale(q02, p[0] + p[2]), scale(p02, -q1), mul(p01, q12), mul(q01, p12))
    e12 = add(scale(q12, p[1] + p[2]), scale(p12, -q0), mul_conj(q02, p01), mul_conj(p02, q01))
    x01 = p01[0] * q01[0] + p01[1] * q01[1]
    x02 = p02[0] * q02[0] + p02[1] * q02[1]
    x12 = p12[0] * q12[0] + p12[1] * q12[1]
    last = p[2] * q2
    return (
        p[0] * q0 - last + x01 - x12,
        p[1] * q1 - last + x01 - x02,
        scale(e01, 0.5),
        scale(e02, 0.5),
        scale(e12, 0.5),
    )


def i_commutator(x, y):
    x0, x1, x01, x02, x12 = x
    y0, y1, y01, y02, y12 = y
    c01 = sub(add(scale(y01, x0 - x1), scale(x01, y1 - y0), mul_conj(x02, y12)), mul_conj(y02, x12))
    c02 = sub(add(scale(y02, x0), scale(x02, -y0), mul(x01, y12)), mul(y01, x12))
    c12 = sub(add(scale(y12, x1), scale(x12, -y1), mul_conj(y02, x01)), mul_conj(x02, y01))
    a01 = x01[1] * y01[0] - x01[0] * y01[1]
    a02 = x02[1] * y02[0] - x02[0] * y02[1]
    a12 = x12[1] * y12[0] - x12[0] * y12[1]
    d2 = 2.0 * (a02 + a12)
    return (
        -2.0 * (a01 + a02) - d2,
        2.0 * (a01 - a12) - d2,
        (-c01[1], c01[0]),
        (-c02[1], c02[0]),
        (-c12[1], c12[0]),
    )


def plane(p):
    mu = jnp.where(p < 3, 0, jnp.where(p < 5, 1, 2))
    nu = jnp.where(p < 3, p + 1, jnp.where(p < 5, p - 1, 3))
    return mu, nu


PLANES = ((0, 1), (0, 2), (0, 3), (1, 2), (1, 3), (2, 3))


def grid_of(shape):
    lane = lax.broadcasted_iota(jnp.int32, shape, 1)
    row = lax.broadcasted_iota(jnp.int32, shape, 0)
    return row, lane


def move_z(v, step):
    row, lane = grid_of(v.shape)
    inside = pltpu.roll(v, (-step) % LANES, 1)
    across = pltpu.roll(v, (step * (NZ - 1)) % LANES, 1)
    edge = NZ - 1 if step > 0 else 0
    return jnp.where(lane % NZ == edge, across, inside)


def move_y(v, step, per_cell):
    rows = v.shape[0]
    row, lane = grid_of(v.shape)
    turned = pltpu.roll(v, (-step * NZ) % LANES, 1)
    inside = pltpu.roll(turned, (-step) % rows, 0)
    across = pltpu.roll(turned, (step * (per_cell - 1)) % rows, 0)
    edge = per_cell - 1 if step > 0 else 0
    other = jnp.where(row % per_cell == edge, across, inside)
    over = lane >= LANES - NZ if step > 0 else lane < NZ
    return jnp.where(over, other, turned)


def load_matrix(ref, index, rows):
    at = lambda c: ref[(*index, c, rows, slice(None))]
    return [[(at(3 * i + j), at(9 + 3 * i + j)) for j in range(3)] for i in range(3)]


def store_matrix(ref, index, rows, m):
    for i in range(3):
        for j in range(3):
            for part in range(2):
                ref[(*index, 9 * part + 3 * i + j, rows, slice(None))] = m[i][j][part]


def load_flat(ref, index, rows):
    return unflat([ref[(*index, c, rows, slice(None))] for c in range(8)])


def store_flat(ref, index, rows, h):
    for c, v in enumerate(flat(h)):
        ref[(*index, c, rows, slice(None))] = v


def add_flat(ref, index, rows, h):
    for c, v in enumerate(flat(h)):
        ref[(*index, c, rows, slice(None))] += v

MESH = pl.DeviceIdType.MESH


class Side:
    def __init__(self, shift, period, shape):
        row, _ = grid_of(shape)
        self.rows = shape[0]
        self.shift = shift
        self.first = row % period < shift

    def turn(self, v, amount):
        return pltpu.roll(v, amount % self.rows, 0)

    def pack_first(self, v0, v1):
        return jnp.where(self.first, v0, self.turn(v1, self.shift))

    def pack_last(self, v0, v1):
        return jnp.where(self.first, self.turn(v0, -self.shift), v1)

    def ahead(self, v0, v1, got):
        s = self.shift
        return (
            jnp.where(self.first, self.turn(v0, -s), self.turn(got, s)),
            jnp.where(self.first, self.turn(v1, -s), got),
        )

    def behind(self, v0, v1, got):
        s = self.shift
        return (
            jnp.where(self.first, got, self.turn(v0, s)),
            jnp.where(self.first, self.turn(got, -s), self.turn(v1, s)),
        )


def chunk_loop(count, fn):
    def step(k, carry):
        fn(pl.ds(pl.multiple_of(8 * k, 8), 8))
        return carry

    lax.fori_loop(0, count, step, 0)


def index_loop(count, fn):
    def step(k, carry):
        fn(k)
        return carry

    lax.fori_loop(0, count, step, 0)


def third_row(full, index, chunks):
    def fn(rows):
        m = [
            [(full[(*index, 3 * i + j, rows, slice(None))], full[(*index, 9 + 3 * i + j, rows, slice(None))]) for j in range(3)]
            for i in range(2)
        ]
        for j, v in enumerate(cross_row(*m)):
            full[(*index, 6 + j, rows, slice(None))] = v[0]
            full[(*index, 15 + j, rows, slice(None))] = v[1]

    chunk_loop(chunks, fn)


X_PLANES = (0, 1, 2)
T_PLANES = (2, 4, 5)


def fused_kernel(
    nx, nt, per_cell, bricks, tms,
    weights, own, target,
    force_out, sums_out,
    full, plaq, here, moved_b, moved_c, res, force,
    link_x, link_x_in, link_t, link_t_in,
    vel_x, vel_x_in, vel_t, vel_t_in,
    res_x, res_x_in, res_t, res_t_in,
    for_x, for_x_in, for_t, for_t_in,
    sums_a, sums_b,
    sent, arrived, sent_a, arrived_a, sent_b, arrived_b,
):
    total = own.shape[2]
    chunks = total // 8
    g, bx, tm = lax.axis_index("groups"), lax.axis_index("brick"), lax.axis_index("tm")
    shape = (total, LANES)
    side_x = Side(nt * per_cell, nx * nt * per_cell, shape)
    side_t = Side(per_cell, nt * per_cell, shape)

    barrier = pltpu.get_barrier_semaphore()
    for k in range(1, bricks):
        pl.semaphore_signal(barrier, inc=1, device_id=(g, lax.rem(bx + k, bricks), tm), device_id_type=MESH)
    for k in range(1, tms):
        pl.semaphore_signal(barrier, inc=1, device_id=(g, bx, lax.rem(tm + k, tms)), device_id_type=MESH)

    x_ahead = (g, lax.rem(bx + 1, bricks), tm)
    x_behind = (g, lax.rem(bx + bricks - 1, bricks), tm)
    t_ahead = (g, bx, lax.rem(tm + 1, tms))
    t_behind = (g, bx, lax.rem(tm + tms - 1, tms))
    copies = []

    def send(src, dst, device):
        n = len(copies)
        copy = pltpu.make_async_remote_copy(
            src_ref=src, dst_ref=dst, send_sem=sent.at[n], recv_sem=arrived.at[n],
            device_id=device, device_id_type=MESH,
        )
        copy.start()
        copies.append(copy)
        return copy

    def pack_links(side, out, base):
        def fn(c):
            for k in range(3):
                out[k, c] = side.pack_first(own[base + k, 2 * c], own[base + k, 2 * c + 1])
        index_loop(6, fn)

    pack_links(side_t, link_t, 0)
    pack_links(side_x, link_x, 1)
    pl.semaphore_wait(barrier, bricks + tms - 2)
    got_link_t = send(link_t, link_t_in, t_behind)
    got_link_x = send(link_x, link_x_in, x_behind)

    for half in range(2):
        def copy_own(c):
            for d in range(4):
                full[0, d, c + 9 * half] = own[d, c + 6 * half]
        index_loop(6, copy_own)
    index_loop(4, lambda d: third_row(full, (0, d), chunks))

    def shift_links(c):
        for d in range(4):
            value = full[0, d, c]
            if d != 1:
                full[2, d, c] = move_y(value, 1, per_cell)
            if d != 2:
                full[3, d, c] = move_z(value, 1)

    index_loop(18, shift_links)

    def loop_plane(p):
        mu, nu = plane(p)

        def fn(rows):
            a = load_matrix(full, (0, mu), rows)
            b = load_matrix(full, (1 + mu, nu), rows)
            c = load_matrix(full, (1 + nu, mu), rows)
            d = load_matrix(full, (0, nu), rows)
            loop = product_dagger(product(a, b), product(d, c))
            store_matrix(plaq, (p,), rows, loop)
            pi = anti_part(loop)
            store_flat(here, (p,), rows, pi)
            store_flat(moved_b, (p,), rows, conjugated(dagger(a), pi))
            store_flat(moved_c, (p,), rows, conjugated(dagger(d), pi))

        chunk_loop(chunks, fn)

    def unpack_links(side, got, base, slot):
        for half in range(2):
            def fn(c):
                for k in range(3):
                    d = base + k
                    n = 2 * c + 9 * half
                    v = side.ahead(full[0, d, n], full[0, d, n + 1], got[k, c + 3 * half])
                    full[slot, d, n], full[slot, d, n + 1] = v
            index_loop(3, fn)
        index_loop(3, lambda k: third_row(full, (slot, base + k), chunks))

    def pack_flat(side, src, p, out, k):
        def fn(c):
            out[k, c] = side.pack_last(src[p, 2 * c], src[p, 2 * c + 1])
        index_loop(4, fn)

    loop_plane(3)
    got_link_x.wait_recv()
    unpack_links(side_x, link_x_in, 1, 1)
    index_loop(2, loop_plane)
    pack_flat(side_x, moved_b, 0, vel_x, 0)
    pack_flat(side_x, moved_b, 1, vel_x, 1)
    got_vel = [send(vel_x.at[k], vel_x_in.at[k], x_ahead) for k in range(2)]
    got_link_t.wait_recv()
    unpack_links(side_t, link_t_in, 0, 4)
    for k, p in enumerate(T_PLANES):
        loop_plane(p)
        pack_flat(side_t, moved_c, p, vel_t, k)
        got_vel.append(send(vel_t.at[k], vel_t_in.at[k], t_ahead))
        if p == 2:
            pack_flat(side_x, moved_b, 2, vel_x, 2)
            got_vel.append(send(vel_x.at[2], vel_x_in.at[2], x_ahead))

    def shift_back(c):
        for p in (3, 4):
            moved_b[p, c] = move_y(moved_b[p, c], -1, per_cell)
        moved_b[5, c] = move_z(moved_b[5, c], -1)
        moved_c[0, c] = move_y(moved_c[0, c], -1, per_cell)
        for p in (1, 3):
            moved_c[p, c] = move_z(moved_c[p, c], -1)

    index_loop(8, shift_back)
    for copy in got_vel:
        copy.wait_recv()

    def unpack_vel(c):
        for k in range(3):
            for side, dst, p, got in ((side_x, moved_b, X_PLANES[k], vel_x_in), (side_t, moved_c, T_PLANES[k], vel_t_in)):
                v = side.behind(dst[p, 2 * c], dst[p, 2 * c + 1], got[k, c])
                dst[p, 2 * c], dst[p, 2 * c + 1] = v

    index_loop(4, unpack_vel)

    def residual_chunk(k, carry):
        rows = pl.ds(pl.multiple_of(8 * k, 8), 8)
        acc = []
        load = lambda ref, index: [ref[index, c, rows, :] for c in range(8)]
        for mu in range(4):
            terms = []
            for nu in range(4):
                if nu == mu:
                    continue
                p = PLANES.index((min(mu, nu), max(mu, nu)))
                sign = 1.0 if mu < nu else -1.0
                terms.append((sign, load(here, p)))
                terms.append((-sign, load(moved_c if mu < nu else moved_b, p)))
            factors = [terms[s][0] * weights[mu, s] for s in range(6)]
            v = [sum(terms[s][1][c] * factors[s] for s in range(6)) for c in range(8)]
            t = [target[mu, a, rows, :] for a in range(8)]
            r3 = v[0] - v[1] - t[2]
            r8 = (v[0] + v[1]) * (1.0 / ROOT_THREE) - t[7]
            r = [
                r3 + ROOT_THREE * r8,
                ROOT_THREE * r8 - r3,
                2.0 * v[2] - t[0],
                2.0 * v[3] + t[1],
                2.0 * v[4] - t[3],
                2.0 * v[5] + t[4],
                2.0 * v[6] - t[5],
                2.0 * v[7] + t[6],
            ]
            for c in range(8):
                res[0, mu, c, rows, :] = r[c]
            part = r8 * (1.0 / ROOT_THREE)
            w = [r3 + part, part - r3] + [2.0 * x for x in r[2:]]
            for sign, term in terms:
                acc.append(sign * sum(w[c] * term[c] for c in range(8)))
        return tuple(x + y for x, y in zip(carry, acc))

    zero = jnp.zeros((8, LANES), jnp.float32)
    acc = lax.fori_loop(0, chunks, residual_chunk, (zero,) * 24)

    def pack_res(side, out, base):
        def fn(c):
            for k in range(3):
                out[k, c] = side.pack_first(res[0, base + k, 2 * c], res[0, base + k, 2 * c + 1])
        index_loop(4, fn)

    pack_res(side_t, res_t, 0)
    got_res_t = send(res_t, res_t_in, t_behind)
    pack_res(side_x, res_x, 1)
    got_res_x = send(res_x, res_x_in, x_behind)

    def share(values, count, me, device_of, sources, sends, arrivals):
        sources[me] = values
        out = []
        for k in range(1, count):
            copy = pltpu.make_async_remote_copy(
                src_ref=sources.at[me], dst_ref=sources.at[me],
                send_sem=sends.at[k - 1], recv_sem=arrivals.at[k - 1],
                device_id=device_of(lax.rem(me + k, count)), device_id_type=MESH,
            )
            copy.start()
            out.append(copy)
        return out

    local = jnp.concatenate([jnp.sum(x, axis=0, keepdims=True) for x in acc], axis=0)
    a_copies = share(local, tms, tm, lambda n: (g, bx, n), sums_a, sent_a, arrived_a)

    def shift_residual(c):
        for d in range(4):
            value = res[0, d, c]
            if d != 1:
                res[2, d, c] = move_y(value, 1, per_cell)
            if d != 2:
                res[3, d, c] = move_z(value, 1)
            force[d, c] = jnp.zeros_like(value)

    index_loop(8, shift_residual)

    def force_plane(p):
        mu, nu = plane(p)
        wa, wc = weights[mu, 2 * (nu - 1)], weights[mu, 2 * (nu - 1) + 1]
        wd, wb = weights[nu, 2 * mu], weights[nu, 2 * mu + 1]

        def fn(rows):
            a = load_matrix(full, (0, mu), rows)
            d = load_matrix(full, (0, nu), rows)
            loop = load_matrix(plaq, (p,), rows)
            pr, pi = hermitian_part(loop), anti_part(loop)
            sb = [x * wb for x in flat(conjugated(a, load_flat(res, (1 + mu, nu), rows)))]
            sc = [x * wc for x in flat(conjugated(d, load_flat(res, (1 + nu, mu), rows)))]
            ra = flat(load_flat(res, (0, mu), rows))
            rd = flat(load_flat(res, (0, nu), rows))
            q = unflat([wa * ra[c] - wd * rd[c] + sb[c] - sc[c] for c in range(8)])
            e = flat(half_anticommutator(pr, q))
            k = [0.5 * x for x in flat(i_commutator(pi, q))]
            fore = [x + y for x, y in zip(e, k)]
            aft = [y - x for x, y in zip(e, k)]
            store_flat(moved_b, (p,), rows, conjugated(dagger(a), unflat(fore)))
            store_flat(moved_c, (p,), rows, conjugated(dagger(d), unflat(aft)))
            xb = flat(i_commutator(pi, unflat(sb)))
            xc = flat(i_commutator(pi, unflat(sc)))
            add_flat(force, (mu,), rows, unflat([x - y for x, y in zip(fore, xb)]))
            add_flat(force, (nu,), rows, unflat([x + y for x, y in zip(aft, xc)]))

        chunk_loop(chunks, fn)

    def unpack_res(side, got, base, slot):
        def fn(c):
            for k in range(3):
                d = base + k
                v = side.ahead(res[0, d, 2 * c], res[0, d, 2 * c + 1], got[k, c])
                res[slot, d, 2 * c], res[slot, d, 2 * c + 1] = v
        index_loop(4, fn)

    force_plane(3)
    for copy in a_copies:
        copy.wait_recv()
    local = sum(sums_a[n] for n in range(tms))
    b_copies = share(local, bricks, bx, lambda n: (g, n, tm), sums_b, sent_b, arrived_b)
    got_res_x.wait_recv()
    unpack_res(side_x, res_x_in, 1, 1)
    index_loop(2, force_plane)
    pack_flat(side_x, moved_b, 0, for_x, 0)
    pack_flat(side_x, moved_b, 1, for_x, 1)
    got_for = [send(for_x.at[k], for_x_in.at[k], x_ahead) for k in range(2)]
    got_res_t.wait_recv()
    unpack_res(side_t, res_t_in, 0, 4)
    for k, p in enumerate(T_PLANES):
        force_plane(p)
        pack_flat(side_t, moved_c, p, for_t, k)
        got_for.append(send(for_t.at[k], for_t_in.at[k], t_ahead))
        if p == 2:
            pack_flat(side_x, moved_b, 2, for_x, 2)
            got_for.append(send(for_x.at[2], for_x_in.at[2], x_ahead))

    def add_back(c):
        force[2, c] += move_y(moved_b[3, c], -1, per_cell)
        force[3, c] += move_y(moved_b[4, c], -1, per_cell) + move_z(moved_b[5, c], -1)
        force[0, c] += move_y(moved_c[0, c], -1, per_cell) + move_z(moved_c[1, c], -1)
        force[1, c] += move_z(moved_c[3, c], -1)

    index_loop(8, add_back)
    for copy in b_copies:
        copy.wait_recv()
    sums_out[...] = sum(sums_b[n] for n in range(bricks))
    for copy in got_for:
        copy.wait_recv()

    def add_far(c):
        for k in range(3):
            for side, src, p, got, d in ((side_x, moved_b, X_PLANES[k], for_x_in, k + 1), (side_t, moved_c, T_PLANES[k], for_t_in, k)):
                v0, v1 = side.behind(src[p, 2 * c], src[p, 2 * c + 1], got[k, c])
                force[d, 2 * c] += v0
                force[d, 2 * c + 1] += v1

    index_loop(4, add_far)

    def write(rows):
        for d in range(4):
            h = [force[d, c, rows, :] for c in range(8)]
            out = [
                2.0 * h[2], -2.0 * h[3], h[0] - h[1], 2.0 * h[4], -2.0 * h[5],
                2.0 * h[6], -2.0 * h[7], (h[0] + h[1]) * (1.0 / ROOT_THREE),
            ]
            for a in range(8):
                force_out[d, a, rows, :] = out[a]

    chunk_loop(chunks, write)
    for copy in copies + a_copies + b_copies:
        copy.wait_send()


def body(link_rows, target, weights):
    f32 = jnp.float32
    nx, nt, plane_sites = link_rows.shape[4:]
    bricks, tms = lax.axis_size("brick"), lax.axis_size("tm")
    sites = nx * nt * plane_sites
    total = sites // LANES
    per_cell = plane_sites // LANES
    space = lambda *lead: pltpu.VMEM((*lead, total, LANES), f32)
    dma = pltpu.SemaphoreType.DMA
    force, sums = pl.pallas_call(
        lambda *refs: fused_kernel(nx, nt, per_cell, bricks, tms, *refs),
        out_shape=(
            jax.ShapeDtypeStruct((4, 8, total, LANES), f32),
            jax.ShapeDtypeStruct((24, LANES), f32),
        ),
        in_specs=[SMEM, VMEM, VMEM],
        out_specs=(VMEM, VMEM),
        scratch_shapes=[
            space(5, 4, 18), space(6, 18), space(6, 8), space(6, 8), space(6, 8),
            space(5, 4, 8), space(4, 8),
            *[space(3, 6)] * 4,
            *[space(3, 4)] * 12,
            pltpu.VMEM((tms, 24, LANES), f32), pltpu.VMEM((bricks, 24, LANES), f32),
            dma((16,)), dma((16,)), dma((tms,)), dma((tms,)), dma((bricks,)), dma((bricks,)),
        ],
        compiler_params=pltpu.CompilerParams(
            vmem_limit_bytes=48 * 1024 * 1024, collective_id=0, has_side_effects=True
        ),
        name="flow",
    )(
        weights,
        link_rows.reshape(4, 12, total, LANES),
        target.reshape(4, 8, total, LANES),
    )
    weight_grad = jnp.sum(sums, axis=1).reshape(4, 6) / (sites * bricks * tms)
    return weight_grad, force.reshape(4, 8, nx, nt, plane_sites)


def solution(mesh):
    in_specs = (
        P("groups", None, None, None, "brick", "tm", None),
        P("groups", None, "brick", "tm", None),
        P(),
    )
    out_specs = (P("groups", None), P("groups", None, "brick", "tm", None))
    return jax.shard_map(body, mesh=mesh, in_specs=in_specs, out_specs=out_specs, check_vma=False)
```

```python
import jax
import jax.numpy as jnp
from jax import lax
from jax.experimental import pallas as pl
from jax.experimental.pallas import tpu as pltpu
from jax.sharding import PartitionSpec as P

NZ = 16
LANES = 128
ROOT_THREE = 3.0**0.5
VMEM = pl.BlockSpec(memory_space=pltpu.VMEM)
SMEM = pl.BlockSpec(memory_space=pltpu.SMEM)


def mul(a, b):
    return a[0] * b[0] - a[1] * b[1], a[0] * b[1] + a[1] * b[0]


def mul_conj(a, b):
    return a[0] * b[0] + a[1] * b[1], a[1] * b[0] - a[0] * b[1]


def add(*terms):
    re, im = terms[0]
    for t in terms[1:]:
        re, im = re + t[0], im + t[1]
    return re, im


def sub(a, b):
    return a[0] - b[0], a[1] - b[1]


def conj(a):
    return a[0], -a[1]


def scale(a, s):
    return a[0] * s, a[1] * s


def cross_row(r, s):
    out = []
    for i, j in ((1, 2), (2, 0), (0, 1)):
        out.append(conj(sub(mul(r[i], s[j]), mul(r[j], s[i]))))
    return out


def product(a, b):
    rows = [
        [add(mul(a[i][0], b[0][k]), mul(a[i][1], b[1][k]), mul(a[i][2], b[2][k])) for k in range(3)]
        for i in range(2)
    ]
    return rows + [cross_row(*rows)]


def product_dagger(a, b):
    rows = [
        [
            add(mul_conj(a[i][0], b[k][0]), mul_conj(a[i][1], b[k][1]), mul_conj(a[i][2], b[k][2]))
            for k in range(3)
        ]
        for i in range(2)
    ]
    return rows + [cross_row(*rows)]


def dagger(a):
    return [[conj(a[j][i]) for j in range(3)] for i in range(3)]


def conjugated(u, h):
    d0, d1, h01, h02, h12 = h
    t = []
    for i in range(2):
        a, b, c = u[i]
        t.append(
            [
                add(scale(a, d0), mul_conj(b, h01), mul_conj(c, h02)),
                add(scale(b, d1), mul(a, h01), mul_conj(c, h12)),
                add(mul(a, h02), mul(b, h12)),
            ]
        )

    def entry(i, j):
        return add(*[mul_conj(t[i][k], u[j][k]) for k in range(3)])

    def diagonal(i):
        return sum(t[i][k][0] * u[i][k][0] + t[i][k][1] * u[i][k][1] for k in range(3))

    e0, e1 = diagonal(0), diagonal(1)
    e2 = d0 + d1 - e0 - e1
    return e0 - e2, e1 - e2, entry(0, 1), entry(0, 2), entry(1, 2)


def flat(h):
    d0, d1, a, b, c = h
    return [d0, d1, *a, *b, *c]


def unflat(v):
    return v[0], v[1], (v[2], v[3]), (v[4], v[5]), (v[6], v[7])


def hermitian_part(p):
    return (
        [p[k][k][0] for k in range(3)],
        *[
            (0.5 * (p[i][j][0] + p[j][i][0]), 0.5 * (p[i][j][1] - p[j][i][1]))
            for i, j in ((0, 1), (0, 2), (1, 2))
        ],
    )


def anti_part(p):
    d = [p[k][k][1] for k in range(3)]
    return (
        d[0] - d[2],
        d[1] - d[2],
        *[
            (0.5 * (p[i][j][1] + p[j][i][1]), 0.5 * (p[j][i][0] - p[i][j][0]))
            for i, j in ((0, 1), (0, 2), (1, 2))
        ],
    )


def half_anticommutator(pr, q):
    p, p01, p02, p12 = pr
    d0, d1, q01, q02, q12 = q
    mean = (d0 + d1) * (1.0 / 3.0)
    q0, q1, q2 = d0 - mean, d1 - mean, -mean
    e01 = add(scale(q01, p[0] + p[1]), scale(p01, -q2), mul_conj(p02, q12), mul_conj(q02, p12))
    e02 = add(scale(q02, p[0] + p[2]), scale(p02, -q1), mul(p01, q12), mul(q01, p12))
    e12 = add(scale(q12, p[1] + p[2]), scale(p12, -q0), mul_conj(q02, p01), mul_conj(p02, q01))
    x01 = p01[0] * q01[0] + p01[1] * q01[1]
    x02 = p02[0] * q02[0] + p02[1] * q02[1]
    x12 = p12[0] * q12[0] + p12[1] * q12[1]
    last = p[2] * q2
    return (
        p[0] * q0 - last + x01 - x12,
        p[1] * q1 - last + x01 - x02,
        scale(e01, 0.5),
        scale(e02, 0.5),
        scale(e12, 0.5),
    )


def i_commutator(x, y):
    x0, x1, x01, x02, x12 = x
    y0, y1, y01, y02, y12 = y
    c01 = sub(add(scale(y01, x0 - x1), scale(x01, y1 - y0), mul_conj(x02, y12)), mul_conj(y02, x12))
    c02 = sub(add(scale(y02, x0), scale(x02, -y0), mul(x01, y12)), mul(y01, x12))
    c12 = sub(add(scale(y12, x1), scale(x12, -y1), mul_conj(y02, x01)), mul_conj(x02, y01))
    a01 = x01[1] * y01[0] - x01[0] * y01[1]
    a02 = x02[1] * y02[0] - x02[0] * y02[1]
    a12 = x12[1] * y12[0] - x12[0] * y12[1]
    d2 = 2.0 * (a02 + a12)
    return (
        -2.0 * (a01 + a02) - d2,
        2.0 * (a01 - a12) - d2,
        (-c01[1], c01[0]),
        (-c02[1], c02[0]),
        (-c12[1], c12[0]),
    )


def plane(p):
    mu = jnp.where(p < 3, 0, jnp.where(p < 5, 1, 2))
    nu = jnp.where(p < 3, p + 1, jnp.where(p < 5, p - 1, 3))
    return mu, nu


PLANES = ((0, 1), (0, 2), (0, 3), (1, 2), (1, 3), (2, 3))


def grid_of(shape):
    lane = lax.broadcasted_iota(jnp.int32, shape, 1)
    row = lax.broadcasted_iota(jnp.int32, shape, 0)
    return row, lane


def move_z(v, step):
    row, lane = grid_of(v.shape)
    inside = pltpu.roll(v, (-step) % LANES, 1)
    across = pltpu.roll(v, (step * (NZ - 1)) % LANES, 1)
    edge = NZ - 1 if step > 0 else 0
    return jnp.where(lane % NZ == edge, across, inside)


def move_y(v, step, per_cell):
    rows = v.shape[0]
    row, lane = grid_of(v.shape)
    turned = pltpu.roll(v, (-step * NZ) % LANES, 1)
    inside = pltpu.roll(turned, (-step) % rows, 0)
    across = pltpu.roll(turned, (step * (per_cell - 1)) % rows, 0)
    edge = per_cell - 1 if step > 0 else 0
    other = jnp.where(row % per_cell == edge, across, inside)
    over = lane >= LANES - NZ if step > 0 else lane < NZ
    return jnp.where(over, other, turned)


def load_matrix(ref, index, rows):
    at = lambda c: ref[(*index, c, rows, slice(None))]
    return [[(at(3 * i + j), at(9 + 3 * i + j)) for j in range(3)] for i in range(3)]


def store_matrix(ref, index, rows, m):
    for i in range(3):
        for j in range(3):
            for part in range(2):
                ref[(*index, 9 * part + 3 * i + j, rows, slice(None))] = m[i][j][part]


def load_flat(ref, index, rows):
    return unflat([ref[(*index, c, rows, slice(None))] for c in range(8)])


def store_flat(ref, index, rows, h):
    for c, v in enumerate(flat(h)):
        ref[(*index, c, rows, slice(None))] = v


def add_flat(ref, index, rows, h):
    for c, v in enumerate(flat(h)):
        ref[(*index, c, rows, slice(None))] += v

MESH = pl.DeviceIdType.MESH


class Side:
    def __init__(self, shift, period, shape):
        row, _ = grid_of(shape)
        self.rows = shape[0]
        self.shift = shift
        self.first = row % period < shift

    def turn(self, v, amount):
        return pltpu.roll(v, amount % self.rows, 0)

    def pack_first(self, v0, v1):
        return jnp.where(self.first, v0, self.turn(v1, self.shift))

    def pack_last(self, v0, v1):
        return jnp.where(self.first, self.turn(v0, -self.shift), v1)

    def ahead(self, v0, v1, got):
        s = self.shift
        return (
            jnp.where(self.first, self.turn(v0, -s), self.turn(got, s)),
            jnp.where(self.first, self.turn(v1, -s), got),
        )

    def behind(self, v0, v1, got):
        s = self.shift
        return (
            jnp.where(self.first, got, self.turn(v0, s)),
            jnp.where(self.first, self.turn(got, -s), self.turn(v1, s)),
        )


def chunk_loop(count, fn):
    def step(k, carry):
        fn(pl.ds(pl.multiple_of(8 * k, 8), 8))
        return carry

    lax.fori_loop(0, count, step, 0)


def index_loop(count, fn):
    def step(k, carry):
        fn(k)
        return carry

    lax.fori_loop(0, count, step, 0)


def third_row(full, index, chunks):
    for k in range(chunks):
        rows = pl.ds(8 * k, 8)
        m = [
            [(full[(*index, 3 * i + j, rows, slice(None))], full[(*index, 9 + 3 * i + j, rows, slice(None))]) for j in range(3)]
            for i in range(2)
        ]
        for j, v in enumerate(cross_row(*m)):
            full[(*index, 6 + j, rows, slice(None))] = v[0]
            full[(*index, 15 + j, rows, slice(None))] = v[1]


T_PLANES = (2, 4, 5)


def fused_kernel(
    nx, nt, per_cell, bricks, tms,
    weights, own, target,
    force_out, sums_out,
    full, plaq, here, moved_b, moved_c, res, force,
    link_x, link_x_in, link_t, link_t_in,
    vel_x, vel_x_in, vel_t, vel_t_in,
    res_x, res_x_in, res_t, res_t_in,
    for_x, for_x_in, for_t, for_t_in,
    sums_a, sums_b,
    sent, arrived, sent_a, arrived_a, sent_b, arrived_b,
):
    total = own.shape[2]
    chunks = total // 8
    g, bx, tm = lax.axis_index("groups"), lax.axis_index("brick"), lax.axis_index("tm")
    shape = (total, LANES)
    side_x = Side(nt * per_cell, nx * nt * per_cell, shape)
    side_t = Side(per_cell, nt * per_cell, shape)

    barrier = pltpu.get_barrier_semaphore()
    for k in range(1, bricks):
        pl.semaphore_signal(barrier, inc=1, device_id=(g, lax.rem(bx + k, bricks), tm), device_id_type=MESH)
    for k in range(1, tms):
        pl.semaphore_signal(barrier, inc=1, device_id=(g, bx, lax.rem(tm + k, tms)), device_id_type=MESH)

    x_ahead = (g, lax.rem(bx + 1, bricks), tm)
    x_behind = (g, lax.rem(bx + bricks - 1, bricks), tm)
    t_ahead = (g, bx, lax.rem(tm + 1, tms))
    t_behind = (g, bx, lax.rem(tm + tms - 1, tms))
    copies = []

    def send(src, dst, device):
        n = len(copies)
        copy = pltpu.make_async_remote_copy(
            src_ref=src, dst_ref=dst, send_sem=sent.at[n], recv_sem=arrived.at[n],
            device_id=device, device_id_type=MESH,
        )
        copy.start()
        copies.append(copy)
        return copy

    def pack_links(side, out, base, k):
        for c in range(6):
            out[k, c] = side.pack_first(own[base + k, 2 * c], own[base + k, 2 * c + 1])

    got_link_t, got_link_x = [None] * 3, [None] * 3
    pack_links(side_t, link_t, 0, 0)
    pl.semaphore_wait(barrier, bricks + tms - 2)
    got_link_t[0] = send(link_t.at[0], link_t_in.at[0], t_behind)
    for out, k in (("x", 2), ("t", 1), ("x", 0), ("t", 2), ("x", 1)):
        if out == "x":
            pack_links(side_x, link_x, 1, k)
            got_link_x[k] = send(link_x.at[k], link_x_in.at[k], x_behind)
        else:
            pack_links(side_t, link_t, 0, k)
            got_link_t[k] = send(link_t.at[k], link_t_in.at[k], t_behind)

    for half in range(2):
        def copy_own(c):
            for d in range(4):
                full[0, d, c + 9 * half] = own[d, c + 6 * half]
        index_loop(6, copy_own)
    index_loop(4, lambda d: third_row(full, (0, d), chunks))

    def shift_links(c):
        for d in range(4):
            value = full[0, d, c]
            if d != 1:
                full[2, d, c] = move_y(value, 1, per_cell)
            if d != 2:
                full[3, d, c] = move_z(value, 1)

    index_loop(18, shift_links)

    def loop_plane(p):
        mu, nu = plane(p)

        def fn(rows):
            a = load_matrix(full, (0, mu), rows)
            b = load_matrix(full, (1 + mu, nu), rows)
            c = load_matrix(full, (1 + nu, mu), rows)
            d = load_matrix(full, (0, nu), rows)
            loop = product_dagger(product(a, b), product(d, c))
            store_matrix(plaq, (p,), rows, loop)
            pi = anti_part(loop)
            store_flat(here, (p,), rows, pi)
            store_flat(moved_b, (p,), rows, conjugated(dagger(a), pi))
            store_flat(moved_c, (p,), rows, conjugated(dagger(d), pi))

        chunk_loop(chunks, fn)

    def unpack_links(side, copy, got, base, slot, k):
        copy[k].wait_recv()
        d = base + k
        for half in range(2):
            for c in range(3):
                n = 2 * c + 9 * half
                v = side.ahead(full[0, d, n], full[0, d, n + 1], got[k, c + 3 * half])
                full[slot, d, n], full[slot, d, n + 1] = v
        third_row(full, (slot, d), chunks)

    def pack_flat(side, src, p, out, k):
        for c in range(4):
            out[k, c] = side.pack_last(src[p, 2 * c], src[p, 2 * c + 1])

    got_vel_x, got_vel_t = [None] * 3, [None] * 3

    def send_x(out, got, copy, k):
        pack_flat(side_x, moved_b, k, out, k)
        copy[k] = send(out.at[k], got.at[k], x_ahead)

    def send_t(out, got, copy, k):
        pack_flat(side_t, moved_c, T_PLANES[k], out, k)
        copy[k] = send(out.at[k], got.at[k], t_ahead)

    loop_plane(3)
    for k in range(3):
        if k == 0:
            unpack_links(side_x, got_link_x, link_x_in, 1, 1, 2)
        unpack_links(side_t, got_link_t, link_t_in, 0, 4, k)
        loop_plane(T_PLANES[k])
        send_t(vel_t, vel_t_in, got_vel_t, k)
        if k == 0:
            send_x(vel_x, vel_x_in, got_vel_x, 2)
        if k < 2:
            unpack_links(side_x, got_link_x, link_x_in, 1, 1, k)
            loop_plane(k)
            send_x(vel_x, vel_x_in, got_vel_x, k)

    def shift_back(c):
        for p in (3, 4):
            moved_b[p, c] = move_y(moved_b[p, c], -1, per_cell)
        moved_b[5, c] = move_z(moved_b[5, c], -1)
        moved_c[0, c] = move_y(moved_c[0, c], -1, per_cell)
        for p in (1, 3):
            moved_c[p, c] = move_z(moved_c[p, c], -1)

    index_loop(8, shift_back)

    def unpack_vel(side, copy, dst, p, got, k):
        copy[k].wait_recv()
        for c in range(4):
            v = side.behind(dst[p, 2 * c], dst[p, 2 * c + 1], got[k, c])
            dst[p, 2 * c], dst[p, 2 * c + 1] = v

    def residual_of(mu):
        def fn(k, carry):
            rows = pl.ds(pl.multiple_of(8 * k, 8), 8)
            load = lambda ref, index: [ref[index, c, rows, :] for c in range(8)]
            terms = []
            for nu in range(4):
                if nu == mu:
                    continue
                p = PLANES.index((min(mu, nu), max(mu, nu)))
                sign = 1.0 if mu < nu else -1.0
                terms.append((sign, load(here, p)))
                terms.append((-sign, load(moved_c if mu < nu else moved_b, p)))
            factors = [terms[s][0] * weights[mu, s] for s in range(6)]
            v = [sum(terms[s][1][c] * factors[s] for s in range(6)) for c in range(8)]
            t = [target[mu, a, rows, :] for a in range(8)]
            r3 = v[0] - v[1] - t[2]
            r8 = (v[0] + v[1]) * (1.0 / ROOT_THREE) - t[7]
            r = [
                r3 + ROOT_THREE * r8,
                ROOT_THREE * r8 - r3,
                2.0 * v[2] - t[0],
                2.0 * v[3] + t[1],
                2.0 * v[4] - t[3],
                2.0 * v[5] + t[4],
                2.0 * v[6] - t[5],
                2.0 * v[7] + t[6],
            ]
            for c in range(8):
                res[0, mu, c, rows, :] = r[c]
            part = r8 * (1.0 / ROOT_THREE)
            w = [r3 + part, part - r3] + [2.0 * x for x in r[2:]]
            return tuple(
                x + sign * sum(w[c] * term[c] for c in range(8)) for x, (sign, term) in zip(carry, terms)
            )

        zero = jnp.zeros((8, LANES), jnp.float32)
        return lax.fori_loop(0, chunks, fn, (zero,) * 6)

    def pack_res(side, out, base, k):
        for c in range(4):
            out[k, c] = side.pack_first(res[0, base + k, 2 * c], res[0, base + k, 2 * c + 1])

    got_res_t, got_res_x = [None] * 3, [None] * 3
    parts = [None] * 4
    for mu in (0, 3, 1, 2):
        if mu < 3:
            unpack_vel(side_t, got_vel_t, moved_c, T_PLANES[mu], vel_t_in, mu)
        if mu > 0:
            unpack_vel(side_x, got_vel_x, moved_b, mu - 1, vel_x_in, mu - 1)
        parts[mu] = residual_of(mu)
        if mu < 3:
            pack_res(side_t, res_t, 0, mu)
            got_res_t[mu] = send(res_t.at[mu], res_t_in.at[mu], t_behind)
        if mu > 0:
            pack_res(side_x, res_x, 1, mu - 1)
            got_res_x[mu - 1] = send(res_x.at[mu - 1], res_x_in.at[mu - 1], x_behind)
    acc = [x for part in parts for x in part]

    def share(values, count, me, device_of, sources, sends, arrivals):
        sources[me] = values
        out = []
        for k in range(1, count):
            copy = pltpu.make_async_remote_copy(
                src_ref=sources.at[me], dst_ref=sources.at[me],
                send_sem=sends.at[k - 1], recv_sem=arrivals.at[k - 1],
                device_id=device_of(lax.rem(me + k, count)), device_id_type=MESH,
            )
            copy.start()
            out.append(copy)
        return out

    local = jnp.concatenate([jnp.sum(x, axis=0, keepdims=True) for x in acc], axis=0)
    a_copies = share(local, tms, tm, lambda n: (g, bx, n), sums_a, sent_a, arrived_a)

    def shift_residual(c):
        for d in range(4):
            value = res[0, d, c]
            if d != 1:
                res[2, d, c] = move_y(value, 1, per_cell)
            if d != 2:
                res[3, d, c] = move_z(value, 1)
            force[d, c] = jnp.zeros_like(value)

    index_loop(8, shift_residual)

    def force_plane(p):
        mu, nu = plane(p)
        wa, wc = weights[mu, 2 * (nu - 1)], weights[mu, 2 * (nu - 1) + 1]
        wd, wb = weights[nu, 2 * mu], weights[nu, 2 * mu + 1]

        def fn(rows):
            a = load_matrix(full, (0, mu), rows)
            d = load_matrix(full, (0, nu), rows)
            loop = load_matrix(plaq, (p,), rows)
            pr, pi = hermitian_part(loop), anti_part(loop)
            sb = [x * wb for x in flat(conjugated(a, load_flat(res, (1 + mu, nu), rows)))]
            sc = [x * wc for x in flat(conjugated(d, load_flat(res, (1 + nu, mu), rows)))]
            ra = flat(load_flat(res, (0, mu), rows))
            rd = flat(load_flat(res, (0, nu), rows))
            q = unflat([wa * ra[c] - wd * rd[c] + sb[c] - sc[c] for c in range(8)])
            e = flat(half_anticommutator(pr, q))
            k = [0.5 * x for x in flat(i_commutator(pi, q))]
            fore = [x + y for x, y in zip(e, k)]
            aft = [y - x for x, y in zip(e, k)]
            store_flat(moved_b, (p,), rows, conjugated(dagger(a), unflat(fore)))
            store_flat(moved_c, (p,), rows, conjugated(dagger(d), unflat(aft)))
            xb = flat(i_commutator(pi, unflat(sb)))
            xc = flat(i_commutator(pi, unflat(sc)))
            add_flat(force, (mu,), rows, unflat([x - y for x, y in zip(fore, xb)]))
            add_flat(force, (nu,), rows, unflat([x + y for x, y in zip(aft, xc)]))

        chunk_loop(chunks, fn)

    def unpack_res(side, copy, got, base, slot, k):
        copy[k].wait_recv()
        d = base + k
        for c in range(4):
            v = side.ahead(res[0, d, 2 * c], res[0, d, 2 * c + 1], got[k, c])
            res[slot, d, 2 * c], res[slot, d, 2 * c + 1] = v

    got_for_x, got_for_t = [None] * 3, [None] * 3
    for k in range(3):
        if k == 0:
            unpack_res(side_x, got_res_x, res_x_in, 1, 1, 2)
        unpack_res(side_t, got_res_t, res_t_in, 0, 4, k)
        force_plane(T_PLANES[k])
        send_t(for_t, for_t_in, got_for_t, k)
        if k == 0:
            send_x(for_x, for_x_in, got_for_x, 2)
        if k < 2:
            unpack_res(side_x, got_res_x, res_x_in, 1, 1, k)
            force_plane(k)
            send_x(for_x, for_x_in, got_for_x, k)
        if k == 1:
            for copy in a_copies:
                copy.wait_recv()
            local = sum(sums_a[n] for n in range(tms))
            b_copies = share(local, bricks, bx, lambda n: (g, n, tm), sums_b, sent_b, arrived_b)
    force_plane(3)

    def add_back(c):
        force[2, c] += move_y(moved_b[3, c], -1, per_cell)
        force[3, c] += move_y(moved_b[4, c], -1, per_cell) + move_z(moved_b[5, c], -1)
        force[0, c] += move_y(moved_c[0, c], -1, per_cell) + move_z(moved_c[1, c], -1)
        force[1, c] += move_z(moved_c[3, c], -1)

    index_loop(8, add_back)
    for copy in b_copies:
        copy.wait_recv()
    sums_out[...] = sum(sums_b[n] for n in range(bricks))

    def add_far(side, copy, src, p, got, d, k):
        copy[k].wait_recv()
        for c in range(4):
            v0, v1 = side.behind(src[p, 2 * c], src[p, 2 * c + 1], got[k, c])
            force[d, 2 * c] += v0
            force[d, 2 * c + 1] += v1

    add_far(side_x, got_for_x, moved_b, 2, for_x_in, 3, 2)
    for k in range(3):
        add_far(side_t, got_for_t, moved_c, T_PLANES[k], for_t_in, k, k)
        if k < 2:
            add_far(side_x, got_for_x, moved_b, k, for_x_in, k + 1, k)

    def write(rows):
        for d in range(4):
            h = [force[d, c, rows, :] for c in range(8)]
            out = [
                2.0 * h[2], -2.0 * h[3], h[0] - h[1], 2.0 * h[4], -2.0 * h[5],
                2.0 * h[6], -2.0 * h[7], (h[0] + h[1]) * (1.0 / ROOT_THREE),
            ]
            for a in range(8):
                force_out[d, a, rows, :] = out[a]

    chunk_loop(chunks, write)
    for copy in copies + a_copies + b_copies:
        copy.wait_send()


def body(link_rows, target, weights):
    f32 = jnp.float32
    nx, nt, plane_sites = link_rows.shape[4:]
    bricks, tms = lax.axis_size("brick"), lax.axis_size("tm")
    sites = nx * nt * plane_sites
    total = sites // LANES
    per_cell = plane_sites // LANES
    space = lambda *lead: pltpu.VMEM((*lead, total, LANES), f32)
    dma = pltpu.SemaphoreType.DMA
    force, sums = pl.pallas_call(
        lambda *refs: fused_kernel(nx, nt, per_cell, bricks, tms, *refs),
        out_shape=(
            jax.ShapeDtypeStruct((4, 8, total, LANES), f32),
            jax.ShapeDtypeStruct((24, LANES), f32),
        ),
        in_specs=[SMEM, VMEM, VMEM],
        out_specs=(VMEM, VMEM),
        scratch_shapes=[
            space(5, 4, 18), space(6, 18), space(6, 8), space(6, 8), space(6, 8),
            space(5, 4, 8), space(4, 8),
            *[space(3, 6)] * 4,
            *[space(3, 4)] * 12,
            pltpu.VMEM((tms, 24, LANES), f32), pltpu.VMEM((bricks, 24, LANES), f32),
            dma((24,)), dma((24,)), dma((tms,)), dma((tms,)), dma((bricks,)), dma((bricks,)),
        ],
        compiler_params=pltpu.CompilerParams(
            vmem_limit_bytes=48 * 1024 * 1024, collective_id=0, has_side_effects=True
        ),
        name="flow",
    )(
        weights,
        link_rows.reshape(4, 12, total, LANES),
        target.reshape(4, 8, total, LANES),
    )
    weight_grad = jnp.sum(sums, axis=1).reshape(4, 6) / (sites * bricks * tms)
    return weight_grad, force.reshape(4, 8, nx, nt, plane_sites)


def solution(mesh):
    in_specs = (
        P("groups", None, None, None, "brick", "tm", None),
        P("groups", None, "brick", "tm", None),
        P(),
    )
    out_specs = (P("groups", None), P("groups", None, "brick", "tm", None))
    return jax.shard_map(body, mesh=mesh, in_specs=in_specs, out_specs=out_specs, check_vma=False)
```

```python
import jax
import jax.numpy as jnp
from jax import lax
from jax.experimental import pallas as pl
from jax.experimental.pallas import tpu as pltpu
from jax.sharding import PartitionSpec as P

NZ = 16
LANES = 128
ROOT_THREE = 3.0**0.5
VMEM = pl.BlockSpec(memory_space=pltpu.VMEM)
SMEM = pl.BlockSpec(memory_space=pltpu.SMEM)


def mul(a, b):
    return a[0] * b[0] - a[1] * b[1], a[0] * b[1] + a[1] * b[0]


def mul_conj(a, b):
    return a[0] * b[0] + a[1] * b[1], a[1] * b[0] - a[0] * b[1]


def add(*terms):
    re, im = terms[0]
    for t in terms[1:]:
        re, im = re + t[0], im + t[1]
    return re, im


def sub(a, b):
    return a[0] - b[0], a[1] - b[1]


def conj(a):
    return a[0], -a[1]


def scale(a, s):
    return a[0] * s, a[1] * s


def cross_row(r, s):
    out = []
    for i, j in ((1, 2), (2, 0), (0, 1)):
        out.append(conj(sub(mul(r[i], s[j]), mul(r[j], s[i]))))
    return out


def product(a, b):
    rows = [
        [add(mul(a[i][0], b[0][k]), mul(a[i][1], b[1][k]), mul(a[i][2], b[2][k])) for k in range(3)]
        for i in range(2)
    ]
    return rows + [cross_row(*rows)]


def product_dagger(a, b):
    rows = [
        [
            add(mul_conj(a[i][0], b[k][0]), mul_conj(a[i][1], b[k][1]), mul_conj(a[i][2], b[k][2]))
            for k in range(3)
        ]
        for i in range(2)
    ]
    return rows + [cross_row(*rows)]


def dagger(a):
    return [[conj(a[j][i]) for j in range(3)] for i in range(3)]


def conjugated(u, h):
    d0, d1, h01, h02, h12 = h
    t = []
    for i in range(2):
        a, b, c = u[i]
        t.append(
            [
                add(scale(a, d0), mul_conj(b, h01), mul_conj(c, h02)),
                add(scale(b, d1), mul(a, h01), mul_conj(c, h12)),
                add(mul(a, h02), mul(b, h12)),
            ]
        )

    def entry(i, j):
        return add(*[mul_conj(t[i][k], u[j][k]) for k in range(3)])

    def diagonal(i):
        return sum(t[i][k][0] * u[i][k][0] + t[i][k][1] * u[i][k][1] for k in range(3))

    e0, e1 = diagonal(0), diagonal(1)
    e2 = d0 + d1 - e0 - e1
    return e0 - e2, e1 - e2, entry(0, 1), entry(0, 2), entry(1, 2)


def flat(h):
    d0, d1, a, b, c = h
    return [d0, d1, *a, *b, *c]


def unflat(v):
    return v[0], v[1], (v[2], v[3]), (v[4], v[5]), (v[6], v[7])


def hermitian_part(p):
    return (
        [p[k][k][0] for k in range(3)],
        *[
            (0.5 * (p[i][j][0] + p[j][i][0]), 0.5 * (p[i][j][1] - p[j][i][1]))
            for i, j in ((0, 1), (0, 2), (1, 2))
        ],
    )


def anti_part(p):
    d = [p[k][k][1] for k in range(3)]
    return (
        d[0] - d[2],
        d[1] - d[2],
        *[
            (0.5 * (p[i][j][1] + p[j][i][1]), 0.5 * (p[j][i][0] - p[i][j][0]))
            for i, j in ((0, 1), (0, 2), (1, 2))
        ],
    )


def half_anticommutator(pr, q):
    p, p01, p02, p12 = pr
    d0, d1, q01, q02, q12 = q
    mean = (d0 + d1) * (1.0 / 3.0)
    q0, q1, q2 = d0 - mean, d1 - mean, -mean
    e01 = add(scale(q01, p[0] + p[1]), scale(p01, -q2), mul_conj(p02, q12), mul_conj(q02, p12))
    e02 = add(scale(q02, p[0] + p[2]), scale(p02, -q1), mul(p01, q12), mul(q01, p12))
    e12 = add(scale(q12, p[1] + p[2]), scale(p12, -q0), mul_conj(q02, p01), mul_conj(p02, q01))
    x01 = p01[0] * q01[0] + p01[1] * q01[1]
    x02 = p02[0] * q02[0] + p02[1] * q02[1]
    x12 = p12[0] * q12[0] + p12[1] * q12[1]
    last = p[2] * q2
    return (
        p[0] * q0 - last + x01 - x12,
        p[1] * q1 - last + x01 - x02,
        scale(e01, 0.5),
        scale(e02, 0.5),
        scale(e12, 0.5),
    )


def i_commutator(x, y):
    x0, x1, x01, x02, x12 = x
    y0, y1, y01, y02, y12 = y
    c01 = sub(add(scale(y01, x0 - x1), scale(x01, y1 - y0), mul_conj(x02, y12)), mul_conj(y02, x12))
    c02 = sub(add(scale(y02, x0), scale(x02, -y0), mul(x01, y12)), mul(y01, x12))
    c12 = sub(add(scale(y12, x1), scale(x12, -y1), mul_conj(y02, x01)), mul_conj(x02, y01))
    a01 = x01[1] * y01[0] - x01[0] * y01[1]
    a02 = x02[1] * y02[0] - x02[0] * y02[1]
    a12 = x12[1] * y12[0] - x12[0] * y12[1]
    d2 = 2.0 * (a02 + a12)
    return (
        -2.0 * (a01 + a02) - d2,
        2.0 * (a01 - a12) - d2,
        (-c01[1], c01[0]),
        (-c02[1], c02[0]),
        (-c12[1], c12[0]),
    )


def plane(p):
    mu = jnp.where(p < 3, 0, jnp.where(p < 5, 1, 2))
    nu = jnp.where(p < 3, p + 1, jnp.where(p < 5, p - 1, 3))
    return mu, nu


PLANES = ((0, 1), (0, 2), (0, 3), (1, 2), (1, 3), (2, 3))


def grid_of(shape):
    lane = lax.broadcasted_iota(jnp.int32, shape, 1)
    row = lax.broadcasted_iota(jnp.int32, shape, 0)
    return row, lane


def move_z(v, step):
    row, lane = grid_of(v.shape)
    inside = pltpu.roll(v, (-step) % LANES, 1)
    across = pltpu.roll(v, (step * (NZ - 1)) % LANES, 1)
    edge = NZ - 1 if step > 0 else 0
    return jnp.where(lane % NZ == edge, across, inside)


def move_y(v, step, per_cell):
    rows = v.shape[0]
    row, lane = grid_of(v.shape)
    turned = pltpu.roll(v, (-step * NZ) % LANES, 1)
    inside = pltpu.roll(turned, (-step) % rows, 0)
    across = pltpu.roll(turned, (step * (per_cell - 1)) % rows, 0)
    edge = per_cell - 1 if step > 0 else 0
    other = jnp.where(row % per_cell == edge, across, inside)
    over = lane >= LANES - NZ if step > 0 else lane < NZ
    return jnp.where(over, other, turned)


def load_matrix(ref, index, rows):
    at = lambda c: ref[(*index, c, rows, slice(None))]
    return [[(at(3 * i + j), at(9 + 3 * i + j)) for j in range(3)] for i in range(3)]


def store_matrix(ref, index, rows, m):
    for i in range(3):
        for j in range(3):
            for part in range(2):
                ref[(*index, 9 * part + 3 * i + j, rows, slice(None))] = m[i][j][part]


def load_flat(ref, index, rows):
    return unflat([ref[(*index, c, rows, slice(None))] for c in range(8)])


def store_flat(ref, index, rows, h):
    for c, v in enumerate(flat(h)):
        ref[(*index, c, rows, slice(None))] = v


def add_flat(ref, index, rows, h):
    for c, v in enumerate(flat(h)):
        ref[(*index, c, rows, slice(None))] += v

MESH = pl.DeviceIdType.MESH


class Side:
    def __init__(self, shift, period, shape):
        row, _ = grid_of(shape)
        self.rows = shape[0]
        self.shift = shift
        self.first = row % period < shift

    def turn(self, v, amount):
        return pltpu.roll(v, amount % self.rows, 0)

    def pack_first(self, v0, v1):
        return jnp.where(self.first, v0, self.turn(v1, self.shift))

    def pack_last(self, v0, v1):
        return jnp.where(self.first, self.turn(v0, -self.shift), v1)

    def ahead(self, v0, v1, got):
        s = self.shift
        return (
            jnp.where(self.first, self.turn(v0, -s), self.turn(got, s)),
            jnp.where(self.first, self.turn(v1, -s), got),
        )

    def behind(self, v0, v1, got):
        s = self.shift
        return (
            jnp.where(self.first, got, self.turn(v0, s)),
            jnp.where(self.first, self.turn(got, -s), self.turn(v1, s)),
        )


def chunk_loop(count, fn):
    def step(k, carry):
        fn(pl.ds(pl.multiple_of(8 * k, 8), 8))
        return carry

    lax.fori_loop(0, count, step, 0)


def index_loop(count, fn):
    def step(k, carry):
        fn(k)
        return carry

    lax.fori_loop(0, count, step, 0)


def third_row(full, index, chunks):
    for k in range(chunks):
        rows = pl.ds(8 * k, 8)
        m = [
            [(full[(*index, 3 * i + j, rows, slice(None))], full[(*index, 9 + 3 * i + j, rows, slice(None))]) for j in range(3)]
            for i in range(2)
        ]
        for j, v in enumerate(cross_row(*m)):
            full[(*index, 6 + j, rows, slice(None))] = v[0]
            full[(*index, 15 + j, rows, slice(None))] = v[1]


T_PLANES = (2, 4, 5)


def fused_kernel(
    nx, nt, per_cell, bricks, tms,
    weights, own, target,
    force_out, sums_out,
    full, plaq, here, moved_b, moved_c, res, force,
    link_x, link_x_in, link_t, link_t_in,
    vel_x, vel_x_in, vel_t, vel_t_in,
    res_x, res_x_in, res_t, res_t_in,
    for_x, for_x_in, for_t, for_t_in,
    sums_a, sums_b,
    sent, arrived, sent_a, arrived_a, sent_b, arrived_b,
):
    total = own.shape[2]
    chunks = total // 8
    g, bx, tm = lax.axis_index("groups"), lax.axis_index("brick"), lax.axis_index("tm")
    shape = (total, LANES)
    side_x = Side(nt * per_cell, nx * nt * per_cell, shape)
    side_t = Side(per_cell, nt * per_cell, shape)

    barrier = pltpu.get_barrier_semaphore()
    for k in range(1, bricks):
        pl.semaphore_signal(barrier, inc=1, device_id=(g, lax.rem(bx + k, bricks), tm), device_id_type=MESH)
    for k in range(1, tms):
        pl.semaphore_signal(barrier, inc=1, device_id=(g, bx, lax.rem(tm + k, tms)), device_id_type=MESH)

    x_ahead = (g, lax.rem(bx + 1, bricks), tm)
    x_behind = (g, lax.rem(bx + bricks - 1, bricks), tm)
    t_ahead = (g, bx, lax.rem(tm + 1, tms))
    t_behind = (g, bx, lax.rem(tm + tms - 1, tms))
    copies = []

    def send(src, dst, device):
        n = len(copies)
        copy = pltpu.make_async_remote_copy(
            src_ref=src, dst_ref=dst, send_sem=sent.at[n], recv_sem=arrived.at[n],
            device_id=device, device_id_type=MESH,
        )
        copy.start()
        copies.append(copy)
        return copy

    def pack_links(side, out, base, k):
        for c in range(6):
            out[k, c] = side.pack_first(own[base + k, 2 * c], own[base + k, 2 * c + 1])

    got_link_t, got_link_x = [None] * 3, [None] * 3
    pack_links(side_t, link_t, 0, 0)
    pl.semaphore_wait(barrier, bricks + tms - 2)
    got_link_t[0] = send(link_t.at[0], link_t_in.at[0], t_behind)
    for out, k in (("x", 0), ("t", 1), ("x", 2), ("t", 2), ("x", 1)):
        if out == "x":
            pack_links(side_x, link_x, 1, k)
            got_link_x[k] = send(link_x.at[k], link_x_in.at[k], x_behind)
        else:
            pack_links(side_t, link_t, 0, k)
            got_link_t[k] = send(link_t.at[k], link_t_in.at[k], t_behind)

    for half in range(2):
        def copy_own(c):
            for d in range(4):
                full[0, d, c + 9 * half] = own[d, c + 6 * half]
        index_loop(6, copy_own)
    index_loop(4, lambda d: third_row(full, (0, d), chunks))

    def shift_links(c):
        for d in range(4):
            value = full[0, d, c]
            if d != 1:
                full[2, d, c] = move_y(value, 1, per_cell)
            if d != 2:
                full[3, d, c] = move_z(value, 1)

    index_loop(18, shift_links)

    def loop_plane(p):
        mu, nu = plane(p)

        def fn(rows):
            a = load_matrix(full, (0, mu), rows)
            b = load_matrix(full, (1 + mu, nu), rows)
            c = load_matrix(full, (1 + nu, mu), rows)
            d = load_matrix(full, (0, nu), rows)
            loop = product_dagger(product(a, b), product(d, c))
            store_matrix(plaq, (p,), rows, loop)
            pi = anti_part(loop)
            store_flat(here, (p,), rows, pi)
            store_flat(moved_b, (p,), rows, conjugated(dagger(a), pi))
            store_flat(moved_c, (p,), rows, conjugated(dagger(d), pi))

        chunk_loop(chunks, fn)

    def unpack_links(side, copy, got, base, slot, k):
        copy[k].wait_recv()
        d = base + k
        for half in range(2):
            for c in range(3):
                n = 2 * c + 9 * half
                v = side.ahead(full[0, d, n], full[0, d, n + 1], got[k, c + 3 * half])
                full[slot, d, n], full[slot, d, n + 1] = v
        third_row(full, (slot, d), chunks)

    def pack_flat(side, src, p, out, k):
        for c in range(4):
            out[k, c] = side.pack_last(src[p, 2 * c], src[p, 2 * c + 1])

    got_vel_x, got_vel_t = [None] * 3, [None] * 3

    def send_x(out, got, copy, k):
        pack_flat(side_x, moved_b, k, out, k)
        copy[k] = send(out.at[k], got.at[k], x_ahead)

    def send_t(out, got, copy, k):
        pack_flat(side_t, moved_c, T_PLANES[k], out, k)
        copy[k] = send(out.at[k], got.at[k], t_ahead)

    for side, k in (("x", 0), ("t", 0), ("x", 1), ("t", 1), ("t", 2)):
        if side == "x":
            unpack_links(side_x, got_link_x, link_x_in, 1, 1, k)
            loop_plane(k)
            send_x(vel_x, vel_x_in, got_vel_x, k)
            continue
        if k == 0:
            unpack_links(side_x, got_link_x, link_x_in, 1, 1, 2)
        unpack_links(side_t, got_link_t, link_t_in, 0, 4, k)
        loop_plane(T_PLANES[k])
        send_t(vel_t, vel_t_in, got_vel_t, k)
        if k == 0:
            send_x(vel_x, vel_x_in, got_vel_x, 2)
    loop_plane(3)

    def shift_back(c):
        for p in (3, 4):
            moved_b[p, c] = move_y(moved_b[p, c], -1, per_cell)
        moved_b[5, c] = move_z(moved_b[5, c], -1)
        moved_c[0, c] = move_y(moved_c[0, c], -1, per_cell)
        for p in (1, 3):
            moved_c[p, c] = move_z(moved_c[p, c], -1)

    index_loop(8, shift_back)

    def unpack_vel(side, copy, dst, p, got, k):
        copy[k].wait_recv()
        for c in range(4):
            v = side.behind(dst[p, 2 * c], dst[p, 2 * c + 1], got[k, c])
            dst[p, 2 * c], dst[p, 2 * c + 1] = v

    def residual_of(mu):
        def fn(k, carry):
            rows = pl.ds(pl.multiple_of(8 * k, 8), 8)
            load = lambda ref, index: [ref[index, c, rows, :] for c in range(8)]
            terms = []
            for nu in range(4):
                if nu == mu:
                    continue
                p = PLANES.index((min(mu, nu), max(mu, nu)))
                sign = 1.0 if mu < nu else -1.0
                terms.append((sign, load(here, p)))
                terms.append((-sign, load(moved_c if mu < nu else moved_b, p)))
            factors = [terms[s][0] * weights[mu, s] for s in range(6)]
            v = [sum(terms[s][1][c] * factors[s] for s in range(6)) for c in range(8)]
            t = [target[mu, a, rows, :] for a in range(8)]
            r3 = v[0] - v[1] - t[2]
            r8 = (v[0] + v[1]) * (1.0 / ROOT_THREE) - t[7]
            r = [
                r3 + ROOT_THREE * r8,
                ROOT_THREE * r8 - r3,
                2.0 * v[2] - t[0],
                2.0 * v[3] + t[1],
                2.0 * v[4] - t[3],
                2.0 * v[5] + t[4],
                2.0 * v[6] - t[5],
                2.0 * v[7] + t[6],
            ]
            for c in range(8):
                res[0, mu, c, rows, :] = r[c]
            part = r8 * (1.0 / ROOT_THREE)
            w = [r3 + part, part - r3] + [2.0 * x for x in r[2:]]
            return tuple(
                x + sign * sum(w[c] * term[c] for c in range(8)) for x, (sign, term) in zip(carry, terms)
            )

        zero = jnp.zeros((8, LANES), jnp.float32)
        return lax.fori_loop(0, chunks, fn, (zero,) * 6)

    def pack_res(side, out, base, k):
        for c in range(4):
            out[k, c] = side.pack_first(res[0, base + k, 2 * c], res[0, base + k, 2 * c + 1])

    got_res_t, got_res_x = [None] * 3, [None] * 3
    parts = [None] * 4
    for mu in (0, 3, 1, 2):
        if mu < 3:
            unpack_vel(side_t, got_vel_t, moved_c, T_PLANES[mu], vel_t_in, mu)
        if mu > 0:
            unpack_vel(side_x, got_vel_x, moved_b, mu - 1, vel_x_in, mu - 1)
        parts[mu] = residual_of(mu)
        if mu < 3:
            pack_res(side_t, res_t, 0, mu)
            got_res_t[mu] = send(res_t.at[mu], res_t_in.at[mu], t_behind)
        if mu > 0:
            pack_res(side_x, res_x, 1, mu - 1)
            got_res_x[mu - 1] = send(res_x.at[mu - 1], res_x_in.at[mu - 1], x_behind)
    acc = [x for part in parts for x in part]

    def share(values, count, me, device_of, sources, sends, arrivals):
        sources[me] = values
        out = []
        for k in range(1, count):
            copy = pltpu.make_async_remote_copy(
                src_ref=sources.at[me], dst_ref=sources.at[me],
                send_sem=sends.at[k - 1], recv_sem=arrivals.at[k - 1],
                device_id=device_of(lax.rem(me + k, count)), device_id_type=MESH,
            )
            copy.start()
            out.append(copy)
        return out

    local = jnp.concatenate([jnp.sum(x, axis=0, keepdims=True) for x in acc], axis=0)
    a_copies = share(local, tms, tm, lambda n: (g, bx, n), sums_a, sent_a, arrived_a)

    def shift_residual(c):
        for d in range(4):
            value = res[0, d, c]
            if d != 1:
                res[2, d, c] = move_y(value, 1, per_cell)
            if d != 2:
                res[3, d, c] = move_z(value, 1)
            force[d, c] = jnp.zeros_like(value)

    index_loop(8, shift_residual)

    def force_plane(p):
        mu, nu = plane(p)
        wa, wc = weights[mu, 2 * (nu - 1)], weights[mu, 2 * (nu - 1) + 1]
        wd, wb = weights[nu, 2 * mu], weights[nu, 2 * mu + 1]

        def fn(rows):
            a = load_matrix(full, (0, mu), rows)
            d = load_matrix(full, (0, nu), rows)
            loop = load_matrix(plaq, (p,), rows)
            pr, pi = hermitian_part(loop), anti_part(loop)
            sb = [x * wb for x in flat(conjugated(a, load_flat(res, (1 + mu, nu), rows)))]
            sc = [x * wc for x in flat(conjugated(d, load_flat(res, (1 + nu, mu), rows)))]
            ra = flat(load_flat(res, (0, mu), rows))
            rd = flat(load_flat(res, (0, nu), rows))
            q = unflat([wa * ra[c] - wd * rd[c] + sb[c] - sc[c] for c in range(8)])
            e = flat(half_anticommutator(pr, q))
            k = [0.5 * x for x in flat(i_commutator(pi, q))]
            fore = [x + y for x, y in zip(e, k)]
            aft = [y - x for x, y in zip(e, k)]
            store_flat(moved_b, (p,), rows, conjugated(dagger(a), unflat(fore)))
            store_flat(moved_c, (p,), rows, conjugated(dagger(d), unflat(aft)))
            xb = flat(i_commutator(pi, unflat(sb)))
            xc = flat(i_commutator(pi, unflat(sc)))
            add_flat(force, (mu,), rows, unflat([x - y for x, y in zip(fore, xb)]))
            add_flat(force, (nu,), rows, unflat([x + y for x, y in zip(aft, xc)]))

        chunk_loop(chunks, fn)

    def unpack_res(side, copy, got, base, slot, k):
        copy[k].wait_recv()
        d = base + k
        for c in range(4):
            v = side.ahead(res[0, d, 2 * c], res[0, d, 2 * c + 1], got[k, c])
            res[slot, d, 2 * c], res[slot, d, 2 * c + 1] = v

    got_for_x, got_for_t = [None] * 3, [None] * 3
    for k in range(3):
        if k == 0:
            unpack_res(side_x, got_res_x, res_x_in, 1, 1, 2)
        unpack_res(side_t, got_res_t, res_t_in, 0, 4, k)
        force_plane(T_PLANES[k])
        send_t(for_t, for_t_in, got_for_t, k)
        if k == 0:
            send_x(for_x, for_x_in, got_for_x, 2)
    for copy in a_copies:
        copy.wait_recv()
    local = sum(sums_a[n] for n in range(tms))
    b_copies = share(local, bricks, bx, lambda n: (g, n, tm), sums_b, sent_b, arrived_b)
    for k in range(2):
        unpack_res(side_x, got_res_x, res_x_in, 1, 1, k)
        force_plane(k)
        send_x(for_x, for_x_in, got_for_x, k)
    force_plane(3)

    def add_back(c):
        force[2, c] += move_y(moved_b[3, c], -1, per_cell)
        force[3, c] += move_y(moved_b[4, c], -1, per_cell) + move_z(moved_b[5, c], -1)
        force[0, c] += move_y(moved_c[0, c], -1, per_cell) + move_z(moved_c[1, c], -1)
        force[1, c] += move_z(moved_c[3, c], -1)

    index_loop(8, add_back)
    for copy in b_copies:
        copy.wait_recv()
    sums_out[...] = sum(sums_b[n] for n in range(bricks))

    def add_far(side, copy, src, p, got, d, k):
        copy[k].wait_recv()
        for c in range(4):
            v0, v1 = side.behind(src[p, 2 * c], src[p, 2 * c + 1], got[k, c])
            force[d, 2 * c] += v0
            force[d, 2 * c + 1] += v1

    add_far(side_x, got_for_x, moved_b, 2, for_x_in, 3, 2)
    for k in range(3):
        add_far(side_t, got_for_t, moved_c, T_PLANES[k], for_t_in, k, k)
    for k in range(2):
        add_far(side_x, got_for_x, moved_b, k, for_x_in, k + 1, k)

    def write(rows):
        for d in range(4):
            h = [force[d, c, rows, :] for c in range(8)]
            out = [
                2.0 * h[2], -2.0 * h[3], h[0] - h[1], 2.0 * h[4], -2.0 * h[5],
                2.0 * h[6], -2.0 * h[7], (h[0] + h[1]) * (1.0 / ROOT_THREE),
            ]
            for a in range(8):
                force_out[d, a, rows, :] = out[a]

    chunk_loop(chunks, write)
    for copy in copies + a_copies + b_copies:
        copy.wait_send()


def body(link_rows, target, weights):
    f32 = jnp.float32
    nx, nt, plane_sites = link_rows.shape[4:]
    bricks, tms = lax.axis_size("brick"), lax.axis_size("tm")
    sites = nx * nt * plane_sites
    total = sites // LANES
    per_cell = plane_sites // LANES
    space = lambda *lead: pltpu.VMEM((*lead, total, LANES), f32)
    dma = pltpu.SemaphoreType.DMA
    force, sums = pl.pallas_call(
        lambda *refs: fused_kernel(nx, nt, per_cell, bricks, tms, *refs),
        out_shape=(
            jax.ShapeDtypeStruct((4, 8, total, LANES), f32),
            jax.ShapeDtypeStruct((24, LANES), f32),
        ),
        in_specs=[SMEM, VMEM, VMEM],
        out_specs=(VMEM, VMEM),
        scratch_shapes=[
            space(5, 4, 18), space(6, 18), space(6, 8), space(6, 8), space(6, 8),
            space(5, 4, 8), space(4, 8),
            *[space(3, 6)] * 4,
            *[space(3, 4)] * 12,
            pltpu.VMEM((tms, 24, LANES), f32), pltpu.VMEM((bricks, 24, LANES), f32),
            dma((24,)), dma((24,)), dma((tms,)), dma((tms,)), dma((bricks,)), dma((bricks,)),
        ],
        compiler_params=pltpu.CompilerParams(
            vmem_limit_bytes=48 * 1024 * 1024, collective_id=0, has_side_effects=True
        ),
        name="flow",
    )(
        weights,
        link_rows.reshape(4, 12, total, LANES),
        target.reshape(4, 8, total, LANES),
    )
    weight_grad = jnp.sum(sums, axis=1).reshape(4, 6) / (sites * bricks * tms)
    return weight_grad, force.reshape(4, 8, nx, nt, plane_sites)


def solution(mesh):
    in_specs = (
        P("groups", None, None, None, "brick", "tm", None),
        P("groups", None, "brick", "tm", None),
        P(),
    )
    out_specs = (P("groups", None), P("groups", None, "brick", "tm", None))
    return jax.shard_map(body, mesh=mesh, in_specs=in_specs, out_specs=out_specs, check_vma=False)
```
